128 devices in a mesh: dom: 128 (over z, x, y, core).
Axes of the slice: x: 4, y: 4, z: 4, core: 2. Of those that a mesh axis runs over, the one named last changes fastest.
Arguments:
- elem_dofs: float32 [56, 9, 32768], P(None, None, 'dom'), may hold values from -6 to 6
- star_mats: float32 [3, 9, 9, 32768], P(None, None, None, 'dom'), may hold values from -1.25 to 1.25
- flux_solver: float32 [2, 4, 9, 9, 32768], P(None, None, None, None, 'dom'), may hold values from -1.5 to 1.5
- stiffness: float32 [3, 56, 56], replicated, may hold values from -0.75 to 0.75
- face_proj: float32 [4, 21, 56], replicated, may hold values from -0.75 to 0.75
- lift_mats: float32 [4, 56, 21], replicated, may hold values from -0.625 to 0.625
- neighbours: int32 [4, 32768], P(None, 'dom'), may hold values from 0 to 32895, as said below
- neighbour_face: int32 [4, 32768], P(None, 'dom'), may hold values from 0 to 3
- cluster: int32 [32768], P('dom'), may hold values from 0 to 3
- fault_elem: int32 [32768], P('dom'), may hold values from 0 to 255, as said below
- fault_face: int32 [32768], P('dom'), may hold values from 0 to 3, as said below
- fault_target: int32 [32768], P('dom'), may hold values from -1 to 32767, as said below
- fault_params: float32 [3, 21, 32768], P(None, None, 'dom'), may hold values from 0.2 to 12, as said below
- fault_state: float32 [21, 32768], P(None, 'dom'), may hold values from 1 to 3
Outputs:
- updated_dofs: float32 [56, 9, 32768], P(None, None, 'dom')
- slip_rate: float32 [21, 32768], P(None, 'dom')
- updated_state: float32 [21, 32768], P(None, 'dom')
The draws below stay inside these ranges and needn't reach their ends.
Inputs may be any that keep to these rules, and one draw needn't show every extreme that they name: `neighbours`: for an element of device i the number lies in [i * 256, (i + 1) * 256 + 2 * 64), and is never the element's own; both ends are reached. `fault_elem`: on each device the live slots name distinct pairs of element and face. `fault_face`: on each device the live slots name distinct pairs of element and face. `fault_target`: A live slot's value t names owner device t // 256 and slot t % 256 there; no t appears twice; on each device the live slots come first, at least three quarters of them, and some device has all 256 live. At most 2 live slots of one device share an owner, and some device sends exactly 2 to some owner; each owner receives from at most 128 devices. `fault_params`: row 0 lies in 0.2 to 0.6, row 1 in 1.5 to 12, row 2 in 0.5 to 2.
All inputs are finite; a program needn't handle non-finite values.
Results may differ from the reference program's by a relative error of at most 0.0003.
Values sent between devices are 32-bit elements; how exact they have to be, the bound alone decides.
A program may use at most 128 MiB of HBM per device.

```python
import jax
import jax.numpy as jnp
from jax import lax

B = 56
Q = 9
FB = 21
ORD = 6
NF = 4
NC = 4
NEWTON = 4
E_DEV = 256
F_DEV = 256
CAP = 2
RIM = 64
ELEMS = 32768
FAULTS = 32768
N_DOM = 128


def fault_layout(key):
    count_key, shift_key, place_key = jax.random.split(key, 3)
    owner_count = F_DEV // CAP
    fixed = jnp.array([N_DOM // 2, N_DOM - 1, 1], jnp.int32)
    perm = jax.random.permutation(shift_key, N_DOM).astype(jnp.int32)
    ranks = jnp.argsort(perm).astype(jnp.int32)
    values = jnp.arange(N_DOM, dtype=jnp.int32)
    is_fixed = jnp.any(values[:, None] == fixed[None, :], axis=1)
    score = jnp.where(is_fixed, N_DOM + values, ranks)
    order = jnp.argsort(score).astype(jnp.int32)
    shifts = jnp.concatenate([fixed, order[:owner_count - 3]])
    full_dev = (N_DOM - 1 - shifts[owner_count - 1]) % N_DOM
    live_count = jax.random.randint(count_key, (N_DOM,), 3 * F_DEV // 4, F_DEV + 1)
    live_count = live_count.at[full_dev].set(F_DEV)
    live_count = live_count.at[(full_dev + 1) % N_DOM].set(3 * F_DEV // 4)
    slot_index = jnp.arange(F_DEV, dtype=jnp.int32)
    source = jnp.arange(N_DOM, dtype=jnp.int32)
    owner_dev = (source[:, None] + shifts[slot_index // CAP][None, :]) % N_DOM
    target = owner_dev * F_DEV + slot_index[None, :]
    target = jnp.where(slot_index[None, :] < live_count[:, None], target, -1)
    device_keys = jax.random.split(place_key, N_DOM)

    def choose(one_key):
        return jax.random.permutation(one_key, NF * E_DEV)[:F_DEV]
    chosen = jax.vmap(choose)(device_keys)
    inner_pick = 1 + jax.random.permutation(device_keys[0], NF * E_DEV - 2)[:F_DEV - 2]
    first_row = jnp.concatenate([jnp.array([NF * E_DEV - 1, 0], jnp.int32), inner_pick.astype(jnp.int32)])
    chosen = chosen.at[0].set(first_row)
    return (target.reshape(-1).astype(jnp.int32), (chosen // NF).reshape(-1).astype(jnp.int32), (chosen % NF).reshape(-1).astype(jnp.int32))


def draw_fault_target(key, part):
    shared = fault_layout(key)
    return shared[0]


def draw_fault_elem(key, part):
    shared = fault_layout(key)
    return shared[1]


def draw_fault_face(key, part):
    shared = fault_layout(key)
    return shared[2]


def draw_neighbours(key, part):
    key = jax.random.fold_in(key, 11)
    offset = jax.random.randint(key, (NF, ELEMS), -RIM, RIM + 1)
    offset = jnp.where(offset == 0, 1, offset)
    numbers = jnp.arange(ELEMS, dtype=jnp.int32)
    local = numbers % E_DEV
    first_row = jnp.where(local == 0, -RIM, jnp.where(local == E_DEV - 1, RIM, offset[0]))
    offset = offset.at[0].set(first_row)
    return (numbers[None, :] + RIM + offset).astype(jnp.int32)


def draw_fault_params(key, part):
    key = jax.random.fold_in(key, 23)
    lower = jnp.array([0.2, 1.5, 0.5], jnp.float32)[:, None, None]
    upper = jnp.array([0.6, 12.0, 2.0], jnp.float32)[:, None, None]
    unit = jax.random.uniform(key, (3, FB, FAULTS), jnp.float32)
    values = lower * jnp.exp(unit * jnp.log(upper / lower))
    return values.astype(jnp.float32)


def with_ends(values, key, least, high):
    longest = values.shape.index(max(values.shape))
    spots = []
    for shift in (0, 1):
        where = [jax.random.randint(jax.random.fold_in(key, axis), (), 0, length) for axis, length in enumerate(values.shape)]
        where[longest] = (where[longest] + shift) % values.shape[longest]
        spots.append(tuple(where))
    return values.at[spots[0]].set(least).at[spots[1]].set(high)


def shard_levels(key, extent, pieces, low, top_value):
    def one(position, blocks):
        steps = jax.random.uniform(jax.random.fold_in(jax.random.fold_in(key, 6), position), (blocks,), jnp.float32, low / len(pieces), top_value / len(pieces))
        return jnp.repeat(jnp.exp(steps), extent[position] // blocks).reshape((-1,) + (1,) * (len(extent) - position - 1))

    gain = one(*pieces[0])
    for cut in pieces[1:]:
        gain = gain * one(*cut)
    return gain


def normal_values(rng, extent, width, most, cuts=(), kind=jnp.bfloat16):
    values = jax.random.normal(rng, extent, jnp.float32) * width
    if len(cuts) > 0:
        values = shard_levels(rng, extent, cuts, -0.22, 0.18) * values
    return jnp.clip(values, min=-most, max=most).astype(kind)


def setup_inputs(seed: int = 0) -> dict:
    splits = jax.random.split(jax.random.key(seed), 15)
    elem_dofs = normal_values(splits[0], (B, Q, ELEMS), 1.0, 6.0, ((2, 128),), jnp.float32)
    star_mats = normal_values(splits[1], (3, Q, Q, ELEMS), (3 * Q) ** -0.5, 1.25, ((3, 128),), jnp.float32)
    flux_solver = normal_values(splits[2], (2, NF, Q, Q, ELEMS), (2 * Q) ** -0.5, 1.5, ((4, 128),), jnp.float32)
    stiffness = normal_values(splits[3], (3, B, B), B ** -0.5, 0.75, (), jnp.float32)
    face_proj = normal_values(splits[4], (NF, FB, B), B ** -0.5, 0.75, (), jnp.float32)
    lift_mats = normal_values(splits[5], (NF, B, FB), (NF * FB) ** -0.5, 0.625, (), jnp.float32)
    neighbours = draw_neighbours(jax.random.fold_in(splits[14], 71), 0)
    neighbour_face = with_ends(jax.random.randint(splits[7], (NF, ELEMS), 0, NF), jax.random.fold_in(splits[7], 1), 0, NF - 1).astype(jnp.int32)
    cluster = with_ends(jax.random.randint(splits[8], (ELEMS,), 0, NC), jax.random.fold_in(splits[8], 1), 0, NC - 1).astype(jnp.int32)
    fault_elem = draw_fault_elem(jax.random.fold_in(splits[14], 71), 0)
    fault_face = draw_fault_face(jax.random.fold_in(splits[14], 71), 0)
    fault_target = draw_fault_target(jax.random.fold_in(splits[14], 71), 0)
    fault_params = draw_fault_params(jax.random.fold_in(splits[14], 71), 0)
    fault_state = jnp.clip(1.0 + 2.0 * jax.random.uniform(splits[13], (FB, FAULTS), jnp.float32) ** shard_levels(splits[13], (FB, FAULTS), ((1, 128),), -0.2, 0.2), 1.0, 3.0)
    return dict(elem_dofs=elem_dofs, star_mats=star_mats, flux_solver=flux_solver, stiffness=stiffness, face_proj=face_proj, lift_mats=lift_mats, neighbours=neighbours, neighbour_face=neighbour_face, cluster=cluster, fault_elem=fault_elem, fault_face=fault_face, fault_target=fault_target, fault_params=fault_params, fault_state=fault_state)


exact_mode = lax.Precision.HIGHEST
base_step = 0.2
steady_state = 0.8

def inverse_sinh(value):
    magnitude = jnp.abs(value)
    result = jnp.log(magnitude + jnp.sqrt(1.0 + magnitude * magnitude))
    return jnp.where(value < 0.0, -result, result)

def derivatives(elem_dofs, stiffness, star_mats):
    node_count, comp_count, elem_count = elem_dofs.shape
    stacked = stiffness.reshape(3 * node_count, node_count)
    taylor = [elem_dofs]
    for degree in range(ORD - 1):
        stiffened = jnp.dot(stacked, taylor[-1].reshape(node_count, comp_count * elem_count), precision=exact_mode, preferred_element_type=jnp.float32)
        stiffened = stiffened.reshape(3, node_count, comp_count, elem_count)
        taylor.append(lax.optimization_barrier(jnp.sum(star_mats[:, None, :, :, :] * stiffened[:, :, None, :, :], axis=(0, 3))))
    return jnp.stack(taylor)

def integrate(taylor):
    levels_out = []
    for level_id in range(NC):
        interval = base_step * 2.0 ** level_id
        weight = 1.0
        summed = jnp.zeros(taylor.shape[1:], jnp.float32)
        for degree in range(ORD):
            weight = weight * interval / (degree + 1)
            summed = summed + weight * taylor[degree]
        levels_out.append(summed)
    return jnp.stack(levels_out, axis=1)

def face_values(elem_dofs, star_mats, stiffness, face_proj, cluster, neighbours, neighbour_face, own_int, ext_int, offset):
    node_count, comp_count, elem_count = elem_dofs.shape
    face_pts = face_proj.shape[1]
    ext_count = ext_int.shape[3]
    lengths = jnp.array([base_step * 2.0 ** level_id for level_id in range(NC)], jnp.float32)
    selector = (cluster[None, :] == jnp.arange(NC, dtype=jnp.int32)[:, None]).astype(jnp.float32)
    elem_step = lax.optimization_barrier(jnp.sum(selector * lengths[:, None], axis=0))
    own_sum = lax.optimization_barrier(jnp.sum(own_int * selector[None, :, None, :], axis=1))
    flipped = jnp.transpose(stiffness, (0, 2, 1)).reshape(3 * node_count, node_count)
    stiffened = jnp.dot(flipped, own_sum.reshape(node_count, comp_count * elem_count), precision=exact_mode, preferred_element_type=jnp.float32)
    stiffened = stiffened.reshape(3, node_count, comp_count, elem_count)
    volume = lax.optimization_barrier(jnp.sum(star_mats[:, None, :, :, :] * stiffened[:, :, None, :, :], axis=(0, 3)))
    projector = face_proj.reshape(NF * face_pts, node_count)
    own_face = jnp.dot(projector, own_sum.reshape(node_count, comp_count * elem_count), precision=exact_mode, preferred_element_type=jnp.float32)
    own_face = own_face.reshape(NF, face_pts, comp_count, elem_count)
    face_table = jnp.dot(projector, ext_int.reshape(node_count, NC * comp_count * ext_count), precision=exact_mode, preferred_element_type=jnp.float32)
    face_table = face_table.reshape(NF, face_pts, NC, comp_count, ext_count).transpose(1, 3, 0, 2, 4)
    face_table = face_table.reshape(face_pts * comp_count, NF * NC * ext_count)
    column = (neighbour_face * NC + cluster[None, :]) * ext_count + (neighbours - offset)
    nb_face = jnp.take(face_table, column.reshape(-1), axis=1)
    nb_face = nb_face.reshape(face_pts, comp_count, NF, elem_count).transpose(2, 0, 1, 3)
    return (elem_step, volume, own_face, nb_face)

def fault_traces(own_face, nb_face, elem_step, fault_elem, fault_face):
    fault_step = elem_step[fault_elem]
    inner_side = jnp.transpose(own_face[fault_face, :, :, fault_elem], (2, 1, 0)) / fault_step
    outer_side = jnp.transpose(nb_face[fault_face, :, :, fault_elem], (2, 1, 0)) / fault_step
    return (inner_side, outer_side, fault_step)

def friction(near_rows, far_rows, params, state_var):
    rate_coef, stress_bg, impedance = (params[0], params[1], params[2])
    locked = 0.5 * (near_rows[1] + far_rows[1]) + impedance * (far_rows[2] - near_rows[2])
    normal = jnp.maximum(stress_bg - 0.5 * (near_rows[0] + far_rows[0]), 1.0)
    strength = normal * rate_coef
    state_gain = 0.5 * jnp.exp(state_var)
    slip_value = jnp.zeros_like(locked)
    for turn in range(NEWTON):
        scaled = state_gain * slip_value
        mismatch = impedance * slip_value + strength * inverse_sinh(scaled) - locked
        tangent = impedance + strength * state_gain / jnp.sqrt(1.0 + scaled * scaled)
        slip_value = slip_value - mismatch / tangent
    traction = locked - impedance * slip_value
    state_next = steady_state + (state_var - steady_state) * jnp.exp(-jnp.abs(slip_value))
    return (traction, slip_value, state_next)

def finish(elem_dofs, flux_solver, lift_mats, volume, own_face, nb_face, inner_side, outer_side, fault_step, traction, slip_value, fault_elem, fault_face, is_live):
    node_count, comp_count, elem_count = elem_dofs.shape
    face_pts = own_face.shape[1]
    imposed = outer_side.at[3].set(traction).at[7].set(inner_side[7] + slip_value)
    imposed = jnp.transpose(imposed * fault_step, (2, 1, 0))
    face_slot = jnp.where(is_live, fault_face, NF)
    nb_face = nb_face.at[face_slot, :, :, fault_elem].set(imposed, mode='drop')
    face_flux = lax.optimization_barrier(jnp.sum(flux_solver[0][:, None] * own_face[:, :, None], axis=3)) + lax.optimization_barrier(jnp.sum(flux_solver[1][:, None] * nb_face[:, :, None], axis=3))
    lifting = jnp.transpose(lift_mats, (1, 0, 2)).reshape(node_count, NF * face_pts)
    surface = jnp.dot(lifting, face_flux.reshape(NF * face_pts, comp_count * elem_count), precision=exact_mode, preferred_element_type=jnp.float32)
    return elem_dofs + volume - surface.reshape(node_count, comp_count, elem_count)

def split_blocks(array):
    shaped = array.reshape(array.shape[:-1] + (N_DOM, array.shape[-1] // N_DOM))
    return jnp.moveaxis(shaped, -2, 0)

def join_blocks(array):
    moved = jnp.moveaxis(array, 0, -2)
    return moved.reshape(moved.shape[:-2] + (moved.shape[-2] * moved.shape[-1],))

def reference(elem_dofs, star_mats, flux_solver, stiffness, face_proj, lift_mats, neighbours, neighbour_face, cluster, fault_elem, fault_face, fault_target, fault_params, fault_state):
    dof_blocks = split_blocks(elem_dofs)
    star_blocks = split_blocks(star_mats)
    flux_blocks = split_blocks(flux_solver)
    nbr_blocks = split_blocks(neighbours)
    side_blocks = split_blocks(neighbour_face)
    cluster_blocks = split_blocks(cluster)
    elem_slots = fault_elem.reshape(N_DOM, F_DEV)
    face_slots = fault_face.reshape(N_DOM, F_DEV)
    target_slots = fault_target.reshape(N_DOM, F_DEV)

    def predict(block_id):
        return integrate(derivatives(dof_blocks[block_id], stiffness, star_blocks[block_id]))
    int_blocks = lax.map(predict, jnp.arange(N_DOM, dtype=jnp.int32))

    def one_block(block_id):
        current = int_blocks[block_id]
        earlier = int_blocks[jnp.maximum(block_id - 1, 0)][..., E_DEV - RIM:] * (block_id > 0).astype(jnp.float32)
        later = int_blocks[jnp.minimum(block_id + 1, N_DOM - 1)][..., :RIM] * (block_id < N_DOM - 1).astype(jnp.float32)
        ext_int = jnp.concatenate([earlier, current, later], axis=3)
        elem_step, volume, own_face, nb_face = face_values(dof_blocks[block_id], star_blocks[block_id], stiffness, face_proj, cluster_blocks[block_id], nbr_blocks[block_id], side_blocks[block_id], current, ext_int, block_id * E_DEV)
        slot_elem = elem_slots[block_id]
        slot_face = face_slots[block_id]
        slot_target = target_slots[block_id]
        is_live = slot_target >= 0
        inner_side, outer_side, fault_step = fault_traces(own_face, nb_face, elem_step, slot_elem, slot_face)
        safe_slot = jnp.maximum(slot_target, 0)
        near_rows = jnp.stack([inner_side[0], inner_side[3], inner_side[7]])
        far_rows = jnp.stack([outer_side[0], outer_side[3], outer_side[7]])
        traction, slip_value, state_next = friction(near_rows, far_rows, fault_params[:, :, safe_slot], fault_state[:, safe_slot])
        updated = finish(dof_blocks[block_id], flux_blocks[block_id], lift_mats, volume, own_face, nb_face, inner_side, outer_side, fault_step, traction, slip_value, slot_elem, slot_face, is_live)
        return (updated, jnp.where(is_live, slip_value, 0.0), state_next)
    updated, slips, states = lax.map(one_block, jnp.arange(N_DOM, dtype=jnp.int32))
    updated_dofs = join_blocks(updated)
    slip_rate = join_blocks(slips)
    state_flat = join_blocks(states)
    where_to = jnp.where(fault_target >= 0, fault_target, FAULTS)
    updated_state = fault_state.at[:, where_to].set(state_flat, mode='drop')
    return (updated_dofs, slip_rate, updated_state)
```

```python
import functools

import jax
import jax.numpy as jnp
from jax import lax
from jax.experimental import pallas as pl
from jax.experimental.pallas import tpu as pltpu
from jax.sharding import PartitionSpec as P

F32, BF16, I32 = jnp.float32, jnp.bfloat16, jnp.int32
MESH = pl.DeviceIdType.MESH
B, Q, FB, ORD, NF, NC, NEWTON = 56, 9, 21, 6, 4, 4, 4
E, RIM = 256, 64
LO, HI = 8, 16
GP = 32
EXT = 384
BASE_STEP, STEADY = 0.2, 0.8
TAUS = [BASE_STEP * 2.0**c for c in range(NC)]


def term_weights(tau):
    out, weight = [], 1.0
    for degree in range(ORD):
        weight = weight * tau / (degree + 1)
        out.append(weight)
    return out


WEIGHTS = [term_weights(tau) for tau in TAUS]


def iota(shape, dim):
    return lax.broadcasted_iota(I32, shape, dim)


def dot(a, b):
    return jnp.dot(a, b, preferred_element_type=F32)


def dot_nt(a, b):
    return lax.dot_general(a, b, (((1,), (1,)), ((), ())), preferred_element_type=F32)


def split2(x):
    high = x.astype(BF16).astype(F32)
    return high, x - high


def split3(x):
    high = x.astype(BF16)
    rest = x - high.astype(F32)
    mid = rest.astype(BF16)
    low = (rest - mid.astype(F32)).astype(BF16)
    return high, mid, low


def stacked(x):
    high, low = split2(x)
    gap = jnp.zeros((8, x.shape[1]), F32)
    half = jnp.concatenate([high, gap, low, gap], axis=0).astype(BF16)
    return jnp.concatenate([half, half], axis=0)


def left_factor(w):
    both = w + pltpu.roll(w, 64, axis=1)
    high, low = split2(both)
    return jnp.concatenate([high.astype(BF16), low.astype(BF16)], axis=1)


def inverse_sinh(value):
    magnitude = jnp.abs(value)
    result = jnp.log(magnitude + jnp.sqrt(1.0 + magnitude * magnitude))
    return jnp.where(value < 0.0, -result, result)


def kernel(
    dofs_h, star_h, flux_h, stiff, proj, lift, nbr, nbr_face, cluster, f_elem, f_face, f_target, params, state,
    out_h, slip_out, state_out,
    x, star, flux, st, wide, pad_sq, s4, st4, f4, l2, mem, own_of, etab, ubuf,
    hsl, hsr, hrl, hrr, halo, amat, gmat, y, of, nb, fx, acc, pp,
    bq, mq, mq2, rq, bp, mp, mp2, rp, bs, ms, ms2, rs,
    in_sem, out_sem, hs_sem, hr_sem, lo_s, lo_r, hi_s, hi_r,
):
    me = lax.axis_index("dom")
    hi, lo = me // LO, me % LO
    n = LO * HI
    left, right = (me + n - 1) % n, (me + 1) % n

    in_copies = [
        pltpu.make_async_copy(dofs_h, x.at[0], in_sem.at[0]),
        pltpu.make_async_copy(star_h, star, in_sem.at[1]),
        pltpu.make_async_copy(flux_h, flux, in_sem.at[2]),
    ]
    for copy in in_copies:
        copy.start()

    barrier = pltpu.get_barrier_semaphore()

    def greet_lo(j, _):
        pl.semaphore_signal(barrier, inc=1, device_id=(hi * LO + (lo + j) % LO,), device_id_type=MESH)
        return 0

    def greet_hi(j, _):
        pl.semaphore_signal(barrier, inc=1, device_id=(((hi + j) % HI) * LO + lo,), device_id_type=MESH)
        return 0

    lax.fori_loop(1, LO, greet_lo, 0)
    lax.fori_loop(1, HI, greet_hi, 0)
    pl.semaphore_signal(barrier, inc=1, device_id=(left,), device_id_type=MESH)
    pl.semaphore_signal(barrier, inc=1, device_id=(right,), device_id_type=MESH)

    def lo_copy(buf, dst, rows, which, j):
        t = (lo + j) % LO
        return pltpu.make_async_remote_copy(
            src_ref=buf.at[pl.ds(pl.multiple_of(t * rows, 8), rows)],
            dst_ref=dst.at[pl.ds(pl.multiple_of(lo * rows, 8), rows)],
            send_sem=lo_s.at[which, j], recv_sem=lo_r.at[which, j],
            device_id=(hi * LO + t,), device_id_type=MESH,
        )

    def hi_copy(buf, dst, rows, which, j):
        t = (hi + j) % HI
        return pltpu.make_async_remote_copy(
            src_ref=buf.at[pl.ds(pl.multiple_of(t * rows, 8), rows)],
            dst_ref=dst.at[pl.ds(pl.multiple_of(hi * rows, 8), rows)],
            send_sem=hi_s.at[which, j], recv_sem=hi_r.at[which, j],
            device_id=(t * LO + lo,), device_id_type=MESH,
        )

    def send(make, count, mine, buf, dst, rows, which):
        def one(j, _):
            make(buf, dst, rows, which, j).start()
            return 0

        lax.fori_loop(1, count, one, 0)
        block = pl.ds(pl.multiple_of(mine * rows, 8), rows)
        dst[block, :] = buf[block, :]

    def arrive(make, count, buf, dst, rows, which):
        def one(j, _):
            make(buf, dst, rows, which, j).wait_recv()
            return 0

        lax.fori_loop(1, count, one, 0)

    def sent(make, count, buf, dst, rows, which):
        def one(j, _):
            make(buf, dst, rows, which, j).wait_send()
            return 0

        lax.fori_loop(1, count, one, 0)

    def halo_copies(k):
        return (
            pltpu.make_async_remote_copy(
                src_ref=hsl.at[k], dst_ref=hrr.at[k], send_sem=hs_sem.at[0, k], recv_sem=hr_sem.at[0, k],
                device_id=(left,), device_id_type=MESH),
            pltpu.make_async_remote_copy(
                src_ref=hsr.at[k], dst_ref=hrl.at[k], send_sem=hs_sem.at[1, k], recv_sem=hr_sem.at[1, k],
                device_id=(right,), device_id_type=MESH),
        )

    wide[...] = jnp.zeros_like(wide)
    for d in range(3):
        wide[d * B : (d + 1) * B, 0:B] = stiff[d]
    s4[...] = left_factor(wide[...])
    for d in range(3):
        pad_sq[...] = jnp.zeros_like(pad_sq)
        pad_sq[0:B, 0:B] = stiff[d]
        wide[d * B : (d + 1) * B, :] = jnp.transpose(pad_sq[...])[0:B]
    st4[...] = left_factor(wide[...])
    pad_sq[...] = jnp.zeros_like(pad_sq)
    for f in range(NF):
        pad_sq[f * GP : f * GP + FB, 0:B] = proj[:, f, :]
    f4[...] = left_factor(pad_sq[...])
    pad_sq[...] = jnp.zeros_like(pad_sq)
    for f in range(NF):
        pad_sq[f * GP : f * GP + FB, 0:B] = lift[:, f, :]
    lift_high, lift_low = split2(jnp.transpose(pad_sq[...])[0:B])
    lift_rows = jnp.concatenate([lift_high, lift_low], axis=0).astype(BF16)
    l2[...] = jnp.concatenate([lift_rows, lift_rows], axis=1)
    fx[...] = jnp.zeros_like(fx)
    pp[...] = jnp.zeros_like(pp)
    for j in range(3):
        pp[24 * j : 24 * j + FB, :] = params[j]
    pp[72 : 72 + FB, :] = state[...]

    target = f_target[...]
    live = target >= 0
    owner = jnp.where(live, lax.shift_right_logical(target, 8), -1)
    slot = jnp.bitwise_and(target, E - 1)
    member = jnp.where(iota((n, E), 0) == owner, 1.0, 0.0)
    earlier = jnp.where(iota((E, E), 0) < iota((E, E), 1), 1.0, 0.0).astype(BF16)
    before = dot(member.astype(BF16), earlier)
    rank = jnp.sum(member * before, axis=0, keepdims=True)
    place = (jnp.bitwise_and(owner, LO - 1) * (2 * HI) + lax.shift_right_logical(owner, 3)).astype(F32) + HI * rank
    place = jnp.where(live, place, -1.0)
    mem[...] = jnp.where(iota((E, E), 0).astype(F32) == place, 1.0, 0.0).astype(BF16)
    grid_place = jnp.where(live, f_face[...] * E + f_elem[...], -1)
    for f in range(NF):
        etab[f * E : (f + 1) * E, :] = jnp.where(iota((E, E), 0) + f * E == grid_place, 1.0, 0.0).astype(BF16)
    ids = jnp.where(iota((128, E), 0) < 2, (slot + 1).astype(F32), 0.0).astype(BF16)
    asked = dot_nt(mem[...], ids).reshape(LO, 2, HI, 128)
    lane3 = iota((LO, HI, 128), 2)
    bq[...] = jnp.where(lane3 == 0, asked[:, 0], asked[:, 1]).reshape(n, 128)

    lane = iota((B, 128), 1)
    low_half = lane < RIM

    def pack_halo(k):
        def one(q, _):
            a, b = x[k, q, :, 0:128], x[k, jnp.minimum(q + 5, Q - 1), :, 0:128]
            hsl[k, q] = jnp.where(low_half, a, pltpu.roll(b, RIM, axis=1))
            a, b = x[k, q, :, 128:256], x[k, jnp.minimum(q + 5, Q - 1), :, 128:256]
            hsr[k, q] = jnp.where(low_half, pltpu.roll(a, RIM, axis=1), b)
            return 0

        lax.fori_loop(0, 5, one, 0)
        for copy in halo_copies(k):
            copy.start()

    def star_products(left_w, source):
        def one(q, _):
            st[q] = dot(left_w[...], stacked(source(q)))[0 : 3 * B]
            return 0

        lax.fori_loop(0, Q, one, 0, unroll=3)

    def star_sum(store):
        def one(g, _):
            for l in range(2):
                lanes = slice(l * 128, (l + 1) * 128)
                total = [jnp.zeros((B, 128), F32) for _ in range(3)]
                for q in range(Q):
                    for d in range(3):
                        value = st[q, d * B : (d + 1) * B, lanes]
                        for i in range(3):
                            total[i] = total[i] + star[g * 3 + i, q, d : d + 1, lanes] * value
                for i in range(3):
                    store(g * 3 + i, lanes, total[i])
            return 0

        lax.fori_loop(0, 3, one, 0)

    def taylor(k):
        star_products(s4, lambda q: x[k - 1, q])

        def store(p, lanes, value):
            x[k, p, :, lanes] = value

        star_sum(store)

    for copy in in_copies[:2]:
        copy.wait()
    pl.semaphore_wait(barrier, LO + HI)
    send(lo_copy, LO, lo, bq, mq, HI, 0)
    pack_halo(0)
    taylor(1)
    pack_halo(1)

    arrive(lo_copy, LO, bq, mq, HI, 0)
    for t in range(HI):
        mq2[t * LO : (t + 1) * LO, :] = mq[pl.ds(t, LO, stride=HI), :]
    send(hi_copy, HI, hi, mq2, rq, LO, 0)
    taylor(2)
    pack_halo(2)

    arrive(hi_copy, HI, mq2, rq, LO, 0)
    wanted = (iota((n, E), 1) + 1).astype(F32)
    for r in range(2):
        own_of[r * n : (r + 1) * n, :] = jnp.where(rq[:, r : r + 1] == wanted, 1.0, 0.0).astype(BF16)
    answer = sum(dot_nt(own_of[...], piece) for piece in split3(pp[...]))
    for t in range(HI):
        for r in range(2):
            bp[t * 16 + r * LO : t * 16 + (r + 1) * LO, :] = answer[r * n + t * LO : r * n + (t + 1) * LO]
    send(hi_copy, HI, hi, bp, mp, 16, 1)
    taylor(3)
    pack_halo(3)

    arrive(hi_copy, HI, bp, mp, 16, 1)
    for t in range(LO):
        for r in range(2):
            mp2[t * 32 + r * HI : t * 32 + (r + 1) * HI, :] = mp[pl.ds(r * LO + t, HI, stride=16), :]
    send(lo_copy, LO, lo, mp2, rp, 32, 1)
    taylor(4)
    pack_halo(4)
    taylor(5)
    pack_halo(5)

    level = cluster[...]

    def by_level(values):
        out = jnp.full((1, E), values[0], F32)
        for c in range(1, NC):
            out = jnp.where(level == c, values[c], out)
        return out

    step = by_level(TAUS)
    own_w = [by_level([WEIGHTS[c][k] for c in range(NC)]) for k in range(ORD)]

    def own_term(q, _):
        total = own_w[0] * x[0, q]
        for k in range(1, ORD):
            total = total + own_w[k] * x[k, q]
        wrapped = stacked(total)
        st[q] = dot(st4[...], wrapped)[0 : 3 * B]
        of[q] = dot(f4[...], wrapped)
        return 0

    lax.fori_loop(0, Q, own_term, 0)

    def store_volume(p, lanes, value):
        acc[p, :, lanes] = x[0, p, :, lanes] + value

    star_sum(store_volume)

    number = nbr[...] - me * E
    ext = jnp.where(number < RIM, number + E, jnp.where(number >= E + RIM, number, number - RIM))
    column = level * EXT + ext
    for f in range(NF):
        def build(c, _, f=f):
            rows = pl.ds(pl.multiple_of(c * E, E), E)
            hit = iota((E, E), 0) + c * E == column[f : f + 1]
            gmat[f, rows, :] = jnp.where(hit, 1.0, 0.0).astype(BF16)
            return 0

        lax.fori_loop(0, NC * EXT // E, build, 0)

    keep_low = jnp.where(me > 0, 1, 0)
    keep_high = jnp.where(me < n - 1, 1, 0)
    keep = jnp.where(lane < RIM, keep_low, keep_high) > 0
    for k in range(ORD):
        for copy in halo_copies(k):
            copy.wait_recv()

        def unpack(q, _, k=k):
            a, b = hrl[k, q], hrr[k, q]
            first = jnp.where(low_half, a, pltpu.roll(b, RIM, axis=1))
            halo[k, q] = jnp.where(keep, first, 0.0)
            second = jnp.where(low_half, pltpu.roll(a, RIM, axis=1), b)
            halo[k, q + 5] = jnp.where(keep, second, 0.0)
            return 0

        lax.fori_loop(0, 5, unpack, 0)

    def integrals(q, _):
        for l in range(3):
            if l < 2:
                terms = [x[k, q, :, l * 128 : (l + 1) * 128] for k in range(ORD)]
            else:
                terms = [halo[k, q] for k in range(ORD)]
            for c in range(NC):
                total = WEIGHTS[c][0] * terms[0]
                for k in range(1, ORD):
                    total = total + WEIGHTS[c][k] * terms[k]
                high, low = split2(total)
                rows = pl.ds(pl.multiple_of(q * 2 * B, 16), 2 * B)
                lanes = slice(c * EXT + l * 128, c * EXT + (l + 1) * 128)
                amat[rows, lanes] = jnp.concatenate([high, low], axis=0).astype(BF16)
        return 0

    lax.fori_loop(0, Q, integrals, 0)

    for f in range(NF):
        y[...] = dot(amat[...], gmat[f])
        side = nbr_face[f : f + 1, :]

        def project(q, _, f=f, side=side):
            base = pl.multiple_of(q * 2 * B, 8)
            value = y[pl.ds(base, B), :] + y[pl.ds(base + B, B), :]
            table = dot(f4[...], stacked(value))
            picked = table[0:24]
            for s in range(1, NF):
                picked = jnp.where(side == s, table[s * GP : s * GP + 24], picked)
            nb[q, f * GP : f * GP + 24, :] = picked
            return 0

        lax.fori_loop(0, Q, project, 0, unroll=3)

    arrive(lo_copy, LO, mp2, rp, 32, 1)
    by_slot = sum(dot(piece, mem[...]) for piece in split3(jnp.transpose(rp[...])))
    by_slot = jnp.where(iota((128, E), 0) == 96, 1.0, by_slot)
    slot_state = by_slot[72:96]
    slot_pieces = split3(by_slot)
    slips = []
    for f in range(NF):
        table = etab[f * E : (f + 1) * E, :]
        grid = sum(dot_nt(piece, table) for piece in slot_pieces)
        rate, stress, imp, var = grid[0:24], grid[24:48], grid[48:72], grid[72:96]
        here = grid[96:97] > 0.5
        imp = jnp.where(imp > 0.0, imp, 1.0)
        rows = slice(f * GP, f * GP + 24)
        inner = [of[p, rows, :] / step for p in (0, 3, 7)]
        outer = [nb[p, rows, :] / step for p in (0, 3, 7)]
        locked = 0.5 * (inner[1] + outer[1]) + imp * (outer[2] - inner[2])
        normal = jnp.maximum(stress - 0.5 * (inner[0] + outer[0]), 1.0)
        strength = normal * rate
        gain = 0.5 * jnp.exp(var)
        slip = jnp.zeros_like(locked)
        for _ in range(NEWTON):
            scaled = gain * slip
            mismatch = imp * slip + strength * inverse_sinh(scaled) - locked
            tangent = imp + strength * gain / jnp.sqrt(1.0 + scaled * scaled)
            slip = slip - mismatch / tangent
        traction = locked - imp * slip
        nb[3, rows, :] = jnp.where(here, step * traction, nb[3, rows, :])
        nb[7, rows, :] = jnp.where(here, step * (inner[2] + slip), nb[7, rows, :])
        slips.append(split3(jnp.where(here, slip, 0.0)))
    slot_slip = jnp.zeros((24, E), F32)
    for f in range(NF):
        for piece in slips[f]:
            slot_slip = slot_slip + dot(piece, etab[f * E : (f + 1) * E, :])
    slip_out[...] = slot_slip[0:FB]
    next_state = STEADY + (slot_state - STEADY) * jnp.exp(-jnp.abs(slot_slip))
    gap8, gap72 = jnp.zeros((8, E), F32), jnp.zeros((72, E), F32)
    wrapped = jnp.concatenate([next_state, gap8, next_state, gap72], axis=0)
    told = sum(dot_nt(mem[...], piece) for piece in split3(wrapped)).reshape(LO, 2, HI, 128)
    bs[...] = jnp.where(lane3 < 32, told[:, 0], told[:, 1]).reshape(n, 128)
    send(lo_copy, LO, lo, bs, ms, HI, 2)

    in_copies[2].wait()

    def fluxes(g, _):
        for l in range(2):
            lanes = slice(l * 128, (l + 1) * 128)
            for f in range(NF):
                rows = slice(f * GP, f * GP + 24)
                total = [jnp.zeros((24, 128), F32) for _ in range(3)]
                for q in range(Q):
                    mine, other = of[q, rows, lanes], nb[q, rows, lanes]
                    for i in range(3):
                        total[i] = total[i] + flux[0, g * 3 + i, q, f : f + 1, lanes] * mine
                        total[i] = total[i] + flux[1, g * 3 + i, q, f : f + 1, lanes] * other
                for i in range(3):
                    fx[g * 3 + i, rows, lanes] = total[i]
        return 0

    lax.fori_loop(0, 3, fluxes, 0)

    arrive(lo_copy, LO, bs, ms, HI, 2)
    for t in range(HI):
        ms2[t * LO : (t + 1) * LO, :] = ms[pl.ds(t, LO, stride=HI), :]
    send(hi_copy, HI, hi, ms2, rs, LO, 2)

    def lifted(p, _):
        high, low = split2(fx[p])
        both = jnp.concatenate([high, low], axis=0).astype(BF16)
        surface = dot(l2[...], both)
        acc[p] = acc[p] - (surface[0:B] + surface[B : 2 * B])
        return 0

    lax.fori_loop(0, Q, lifted, 0, unroll=3)
    out_copy = pltpu.make_async_copy(acc, out_h, out_sem)
    out_copy.start()

    arrive(hi_copy, HI, ms2, rs, LO, 2)
    turned = jnp.transpose(rs[...])
    news = jnp.concatenate([turned[0:24], turned[32:56]], axis=1)
    update = sum(dot(piece, own_of[...]) for piece in split3(news))
    hit = dot(jnp.ones((16, E), BF16), own_of[...])[0:1] > 0.5
    state_out[...] = jnp.where(hit, update[0:FB], state[...])

    sent(lo_copy, LO, bq, mq, HI, 0)
    sent(hi_copy, HI, mq2, rq, LO, 0)
    sent(hi_copy, HI, bp, mp, 16, 1)
    sent(lo_copy, LO, mp2, rp, 32, 1)
    sent(lo_copy, LO, bs, ms, HI, 2)
    sent(hi_copy, HI, ms2, rs, LO, 2)
    for k in range(ORD):
        for copy in halo_copies(k):
            copy.wait_send()
    out_copy.wait()


def local(*args):
    (elem_dofs, star_mats, flux_solver, stiffness, face_proj, lift_mats, neighbours, neighbour_face,
     cluster, fault_elem, fault_face, fault_target, fault_params, fault_state) = args
    vmem, anywhere = pl.BlockSpec(memory_space=pltpu.VMEM), pl.BlockSpec(memory_space=pl.ANY)
    halo = pltpu.VMEM((ORD, 5, B, 128), F32)
    small = pltpu.VMEM((LO * HI, 128), F32)
    double = pltpu.VMEM((2 * LO * HI, 128), F32)
    faces = pltpu.VMEM((Q, NF * GP, E), F32)
    square = pltpu.VMEM((E, E), BF16)
    out, slip, state = pl.pallas_call(
        kernel,
        out_shape=(
            jax.ShapeDtypeStruct((Q, B, E), F32),
            jax.ShapeDtypeStruct((FB, E), F32),
            jax.ShapeDtypeStruct((FB, E), F32),
        ),
        in_specs=[anywhere] * 3 + [vmem] * 11,
        out_specs=(anywhere, vmem, vmem),
        scratch_shapes=[
            pltpu.VMEM((ORD, Q, B, E), F32),
            pltpu.VMEM((Q, Q, 3, E), F32),
            pltpu.VMEM((2, Q, Q, NF, E), F32),
            pltpu.VMEM((Q, 3 * B, E), F32),
            pltpu.VMEM((176, 128), F32),
            pltpu.VMEM((128, 128), F32),
            pltpu.VMEM((176, 256), BF16),
            pltpu.VMEM((176, 256), BF16),
            pltpu.VMEM((128, 256), BF16),
            pltpu.VMEM((112, 256), BF16),
            square,
            square,
            pltpu.VMEM((NF * E, E), BF16),
            pltpu.VMEM((8, 128), F32),
            halo, halo, halo, halo,
            pltpu.VMEM((ORD, 10, B, 128), F32),
            pltpu.VMEM((Q * 2 * B, NC * EXT), BF16),
            pltpu.VMEM((NF, NC * EXT, E), BF16),
            pltpu.VMEM((Q * 2 * B, E), F32),
            faces, faces, faces,
            pltpu.VMEM((Q, B, E), F32),
            pltpu.VMEM((128, E), F32),
            small, small, small, small,
            double, double, double, double,
            small, small, small, small,
            pltpu.SemaphoreType.DMA((3,)),
            pltpu.SemaphoreType.DMA,
            pltpu.SemaphoreType.DMA((2, ORD)),
            pltpu.SemaphoreType.DMA((2, ORD)),
            pltpu.SemaphoreType.DMA((3, LO)),
            pltpu.SemaphoreType.DMA((3, LO)),
            pltpu.SemaphoreType.DMA((3, HI)),
            pltpu.SemaphoreType.DMA((3, HI)),
        ],
        compiler_params=pltpu.CompilerParams(
            collective_id=0, has_side_effects=True, vmem_limit_bytes=48 * 1024 * 1024
        ),
    )(
        jnp.transpose(elem_dofs, (1, 0, 2)),
        jnp.transpose(star_mats, (1, 2, 0, 3)),
        jnp.transpose(flux_solver, (0, 2, 3, 1, 4)),
        stiffness,
        jnp.transpose(face_proj, (1, 0, 2)),
        jnp.transpose(lift_mats, (2, 0, 1)),
        neighbours,
        neighbour_face,
        cluster.reshape(1, E),
        fault_elem.reshape(1, E),
        fault_face.reshape(1, E),
        fault_target.reshape(1, E),
        fault_params,
        fault_state,
    )
    return jnp.transpose(out, (1, 0, 2)), slip, state


def solution(mesh):
    return jax.shard_map(
        local,
        mesh=mesh,
        in_specs=(
            P(None, None, "dom"),
            P(None, None, None, "dom"),
            P(None, None, None, None, "dom"),
            P(),
            P(),
            P(),
            P(None, "dom"),
            P(None, "dom"),
            P("dom"),
            P("dom"),
            P("dom"),
            P("dom"),
            P(None, None, "dom"),
            P(None, "dom"),
        ),
        out_specs=(P(None, None, "dom"), P(None, "dom"), P(None, "dom")),
        check_vma=False,
    )
```

```python
import functools

import jax
import jax.numpy as jnp
from jax import lax
from jax.experimental import pallas as pl
from jax.experimental.pallas import tpu as pltpu
from jax.sharding import PartitionSpec as P

F32, BF16, I32 = jnp.float32, jnp.bfloat16, jnp.int32
MESH = pl.DeviceIdType.MESH
B, Q, FB, ORD, NF, NC, NEWTON = 56, 9, 21, 6, 4, 4, 4
E, RIM = 256, 64
LO, HI = 8, 16
GP = 32
EXT = 384
BASE_STEP, STEADY = 0.2, 0.8
TAUS = [BASE_STEP * 2.0**c for c in range(NC)]


def term_weights(tau):
    out, weight = [], 1.0
    for degree in range(ORD):
        weight = weight * tau / (degree + 1)
        out.append(weight)
    return out


WEIGHTS = [term_weights(tau) for tau in TAUS]


def iota(shape, dim):
    return lax.broadcasted_iota(I32, shape, dim)


def dot(a, b):
    return jnp.dot(a, b, preferred_element_type=F32)


def dot_nt(a, b):
    return lax.dot_general(a, b, (((1,), (1,)), ((), ())), preferred_element_type=F32)


def split2(x):
    high = x.astype(BF16).astype(F32)
    return high, x - high


def split3(x):
    high = x.astype(BF16)
    rest = x - high.astype(F32)
    mid = rest.astype(BF16)
    low = (rest - mid.astype(F32)).astype(BF16)
    return high, mid, low


def stacked(x):
    high, low = split2(x)
    gap = jnp.zeros((8, x.shape[1]), F32)
    half = jnp.concatenate([high, gap, low, gap], axis=0).astype(BF16)
    return jnp.concatenate([half, half], axis=0)


def left_factor(w):
    both = w + pltpu.roll(w, 64, axis=1)
    high, low = split2(both)
    return jnp.concatenate([high.astype(BF16), low.astype(BF16)], axis=1)


def inverse_sinh(value):
    magnitude = jnp.abs(value)
    result = jnp.log(magnitude + jnp.sqrt(1.0 + magnitude * magnitude))
    return jnp.where(value < 0.0, -result, result)


def kernel(
    dofs_h, star_h, flux_h, *rest
):
    small_h, rest = rest[:11], rest[11:]
    (out_h, slip_h, state_h), rest = rest[:3], rest[3:]
    small_v, rest = rest[:11], rest[11:]
    stiff, proj, lift, nbr, nbr_face, cluster, f_elem, f_face, f_target, params, state = small_v
    (slip_out, state_out, x, star, flux, st, wide, pad_sq, s4, st4, f4, f4b, l2, mem, own_of, etab,
    hsl, hsr, hrl, hrr, amat, gmat, y, of, nb, fx, acc, pp,
    bq, mq, mq2, rq, bp, mp, mp2, rp, bs, ms, ms2, rs,
    in_sem, out_sem, hs_sem, hr_sem, lo_s, lo_r, hi_s, hi_r) = rest
    me = lax.axis_index("dom")
    hi, lo = me // LO, me % LO
    n = LO * HI
    left, right = (me + n - 1) % n, (me + 1) % n

    in_copies = [
        pltpu.make_async_copy(dofs_h, x.at[0], in_sem.at[0]),
        pltpu.make_async_copy(star_h, star, in_sem.at[1]),
        pltpu.make_async_copy(flux_h, flux, in_sem.at[2]),
    ]
    small_copies = [
        pltpu.make_async_copy(source, place, in_sem.at[3 + i])
        for i, (source, place) in enumerate(zip(small_h, small_v))
    ]
    for copy in small_copies + in_copies:
        copy.start()

    barrier = pltpu.get_barrier_semaphore()

    def greet_lo(j, _):
        pl.semaphore_signal(barrier, inc=1, device_id=(hi * LO + (lo + j) % LO,), device_id_type=MESH)
        return 0

    def greet_hi(j, _):
        pl.semaphore_signal(barrier, inc=1, device_id=(((hi + j) % HI) * LO + lo,), device_id_type=MESH)
        return 0

    lax.fori_loop(1, LO, greet_lo, 0)
    lax.fori_loop(1, HI, greet_hi, 0)
    pl.semaphore_signal(barrier, inc=1, device_id=(left,), device_id_type=MESH)
    pl.semaphore_signal(barrier, inc=1, device_id=(right,), device_id_type=MESH)

    def lo_copy(buf, dst, rows, which, j):
        t = (lo + j) % LO
        return pltpu.make_async_remote_copy(
            src_ref=buf.at[pl.ds(pl.multiple_of(t * rows, 8), rows)],
            dst_ref=dst.at[pl.ds(pl.multiple_of(lo * rows, 8), rows)],
            send_sem=lo_s.at[which, j], recv_sem=lo_r.at[which, j],
            device_id=(hi * LO + t,), device_id_type=MESH,
        )

    def hi_copy(buf, dst, rows, which, j):
        t = (hi + j) % HI
        return pltpu.make_async_remote_copy(
            src_ref=buf.at[pl.ds(pl.multiple_of(t * rows, 8), rows)],
            dst_ref=dst.at[pl.ds(pl.multiple_of(hi * rows, 8), rows)],
            send_sem=hi_s.at[which, j], recv_sem=hi_r.at[which, j],
            device_id=(t * LO + lo,), device_id_type=MESH,
        )

    def send(make, count, mine, buf, dst, rows, which):
        def one(j, _):
            make(buf, dst, rows, which, j).start()
            return 0

        lax.fori_loop(1, count, one, 0)
        block = pl.ds(pl.multiple_of(mine * rows, 8), rows)
        dst[block, :] = buf[block, :]

    def arrive(make, count, buf, dst, rows, which):
        def one(j, _):
            make(buf, dst, rows, which, j).wait_recv()
            return 0

        lax.fori_loop(1, count, one, 0)

    def sent(make, count, buf, dst, rows, which):
        def one(j, _):
            make(buf, dst, rows, which, j).wait_send()
            return 0

        lax.fori_loop(1, count, one, 0)

    def halo_copies(k):
        return (
            pltpu.make_async_remote_copy(
                src_ref=hsl.at[k], dst_ref=hrr.at[k], send_sem=hs_sem.at[0, k], recv_sem=hr_sem.at[0, k],
                device_id=(left,), device_id_type=MESH),
            pltpu.make_async_remote_copy(
                src_ref=hsr.at[k], dst_ref=hrl.at[k], send_sem=hs_sem.at[1, k], recv_sem=hr_sem.at[1, k],
                device_id=(right,), device_id_type=MESH),
        )

    for copy in small_copies:
        copy.wait()
    wide[...] = jnp.zeros_like(wide)
    for d in range(3):
        wide[d * B : (d + 1) * B, 0:B] = stiff[d]
    s4[...] = left_factor(wide[...])
    for d in range(3):
        pad_sq[...] = jnp.zeros_like(pad_sq)
        pad_sq[0:B, 0:B] = stiff[d]
        wide[d * B : (d + 1) * B, :] = jnp.transpose(pad_sq[...])[0:B]
    st4[...] = left_factor(wide[...])
    pad_sq[...] = jnp.zeros_like(pad_sq)
    for f in range(NF):
        pad_sq[f * GP : f * GP + FB, 0:B] = proj[:, f, :]
    f4[...] = left_factor(pad_sq[...])
    high, low = [jnp.concatenate([v, jnp.zeros((128, 128), F32)], axis=1) for v in split2(pad_sq[...])]
    f4b[...] = (
        high + pltpu.roll(high, B, axis=1) + pltpu.roll(low, 2 * B, axis=1) + pltpu.roll(low, 3 * B, axis=1)
    ).astype(BF16)
    pad_sq[...] = jnp.zeros_like(pad_sq)
    for f in range(NF):
        pad_sq[f * GP : f * GP + FB, 0:B] = lift[:, f, :]
    lift_high, lift_low = split2(jnp.transpose(pad_sq[...])[0:B])
    lift_rows = jnp.concatenate([lift_high, lift_low], axis=0).astype(BF16)
    l2[...] = jnp.concatenate([lift_rows, lift_rows], axis=1)
    fx[...] = jnp.zeros_like(fx)
    pp[...] = jnp.zeros_like(pp)
    for j in range(3):
        pp[24 * j : 24 * j + FB, :] = params[j]
    pp[72 : 72 + FB, :] = state[...]

    target = f_target[...]
    live = target >= 0
    owner = jnp.where(live, lax.shift_right_logical(target, 8), -1)
    slot = jnp.bitwise_and(target, E - 1)
    member = jnp.where(iota((n, E), 0) == owner, 1.0, 0.0)
    earlier = jnp.where(iota((E, E), 0) < iota((E, E), 1), 1.0, 0.0).astype(BF16)
    before = dot(member.astype(BF16), earlier)
    rank = jnp.sum(member * before, axis=0, keepdims=True)
    place = (jnp.bitwise_and(owner, LO - 1) * (2 * HI) + lax.shift_right_logical(owner, 3)).astype(F32) + HI * rank
    place = jnp.where(live, place, -1.0)
    mem[...] = jnp.where(iota((E, E), 0).astype(F32) == place, 1.0, 0.0).astype(BF16)
    grid_place = jnp.where(live, f_face[...] * E + f_elem[...], -1)
    for f in range(NF):
        etab[f * E : (f + 1) * E, :] = jnp.where(iota((E, E), 0) + f * E == grid_place, 1.0, 0.0).astype(BF16)
    ids = jnp.where(iota((128, E), 0) < 2, (slot + 1).astype(F32), 0.0).astype(BF16)
    asked = dot_nt(mem[...], ids).reshape(LO, 2, HI, 128)
    lane3 = iota((LO, HI, 128), 2)
    bq[...] = jnp.where(lane3 == 0, asked[:, 0], asked[:, 1]).reshape(n, 128)

    lane = iota((B, 128), 1)
    low_half = lane < RIM

    def pack_halo(k):
        def one(q, _):
            a, b = x[k, q, :, 0:128], x[k, jnp.minimum(q + 5, Q - 1), :, 0:128]
            hsl[k, q] = jnp.where(low_half, a, pltpu.roll(b, RIM, axis=1))
            a, b = x[k, q, :, 128:256], x[k, jnp.minimum(q + 5, Q - 1), :, 128:256]
            hsr[k, q] = jnp.where(low_half, pltpu.roll(a, RIM, axis=1), b)
            return 0

        lax.fori_loop(0, 5, one, 0)
        for copy in halo_copies(k):
            copy.start()

    def star_products(left_w, source):
        def one(q, _):
            st[q] = dot(left_w[...], stacked(source(q)))[0 : 3 * B]
            return 0

        lax.fori_loop(0, Q, one, 0, unroll=True)

    def star_sum(store):
        def one(g, _):
            for l in range(2):
                lanes = slice(l * 128, (l + 1) * 128)
                total = [jnp.zeros((B, 128), F32) for _ in range(3)]
                for q in range(Q):
                    for d in range(3):
                        value = st[q, d * B : (d + 1) * B, lanes]
                        for i in range(3):
                            total[i] = total[i] + star[g * 3 + i, q, d : d + 1, lanes] * value
                for i in range(3):
                    store(g * 3 + i, lanes, total[i])
            return 0

        lax.fori_loop(0, 3, one, 0)

    def taylor(k):
        star_products(s4, lambda q: x[k - 1, q])

        def store(p, lanes, value):
            x[k, p, :, lanes] = value

        star_sum(store)

    for copy in in_copies[:2]:
        copy.wait()
    taylor(1)
    pl.semaphore_wait(barrier, LO + HI)
    send(lo_copy, LO, lo, bq, mq, HI, 0)
    pack_halo(0)
    pack_halo(1)
    taylor(2)
    pack_halo(2)
    taylor(3)
    pack_halo(3)

    arrive(lo_copy, LO, bq, mq, HI, 0)
    for t in range(HI):
        mq2[t * LO : (t + 1) * LO, :] = mq[pl.ds(t, LO, stride=HI), :]
    send(hi_copy, HI, hi, mq2, rq, LO, 0)
    taylor(4)
    pack_halo(4)
    taylor(5)
    pack_halo(5)

    level = cluster[...]

    def by_level(values):
        out = jnp.full((1, E), values[0], F32)
        for c in range(1, NC):
            out = jnp.where(level == c, values[c], out)
        return out

    step = by_level(TAUS)
    own_w = [by_level([WEIGHTS[c][k] for c in range(NC)]) for k in range(ORD)]

    def own_term(q, _):
        total = own_w[0] * x[0, q]
        for k in range(1, ORD):
            total = total + own_w[k] * x[k, q]
        wrapped = stacked(total)
        st[q] = dot(st4[...], wrapped)[0 : 3 * B]
        of[q] = dot(f4[...], wrapped)
        return 0

    lax.fori_loop(0, Q, own_term, 0, unroll=3)

    arrive(hi_copy, HI, mq2, rq, LO, 0)
    wanted = (iota((n, E), 1) + 1).astype(F32)
    for r in range(2):
        own_of[r * n : (r + 1) * n, :] = jnp.where(rq[:, r : r + 1] == wanted, 1.0, 0.0).astype(BF16)
    answer = sum(dot_nt(own_of[...], piece) for piece in split3(pp[...]))
    for t in range(HI):
        for r in range(2):
            bp[t * 16 + r * LO : t * 16 + (r + 1) * LO, :] = answer[r * n + t * LO : r * n + (t + 1) * LO]
    send(hi_copy, HI, hi, bp, mp, 16, 1)

    def store_volume(p, lanes, value):
        acc[p, :, lanes] = x[0, p, :, lanes] + value

    star_sum(store_volume)

    number = nbr[...] - me * E
    ext = jnp.where(number < RIM, number + E, jnp.where(number >= E + RIM, number, number - RIM))
    column = level * EXT + ext
    for f in range(NF):
        def build(c, _, f=f):
            rows = pl.ds(pl.multiple_of(c * E, E), E)
            hit = iota((E, E), 0) + c * E == column[f : f + 1]
            gmat[f, rows, :] = jnp.where(hit, 1.0, 0.0).astype(BF16)
            return 0

        lax.fori_loop(0, NC * EXT // E, build, 0)

    def cluster_sums(terms, row, l):
        for c in range(NC):
            total = WEIGHTS[c][0] * terms[0]
            for k in range(1, ORD):
                total = total + WEIGHTS[c][k] * terms[k]
            high, low = split2(total)
            rows = pl.ds(pl.multiple_of(row * 2 * B, 16), 2 * B)
            lanes = slice(c * EXT + l * 128, c * EXT + (l + 1) * 128)
            amat[rows, lanes] = jnp.concatenate([high, low], axis=0).astype(BF16)

    def own_integrals(q, _):
        for l in range(2):
            cluster_sums([x[k, q, :, l * 128 : (l + 1) * 128] for k in range(ORD)], q, l)
        return 0

    lax.fori_loop(0, Q, own_integrals, 0)

    arrive(hi_copy, HI, bp, mp, 16, 1)
    for t in range(LO):
        for r in range(2):
            mp2[t * 32 + r * HI : t * 32 + (r + 1) * HI, :] = mp[pl.ds(r * LO + t, HI, stride=16), :]
    send(lo_copy, LO, lo, mp2, rp, 32, 1)

    keep_low = jnp.where(me > 0, 1, 0)
    keep_high = jnp.where(me < n - 1, 1, 0)
    keep = jnp.where(lane < RIM, keep_low, keep_high) > 0
    for k in range(ORD):
        for copy in halo_copies(k):
            copy.wait_recv()

    def rim_integrals(q, _):
        first, second = [], []
        for k in range(ORD):
            a, b = hrl[k, q], hrr[k, q]
            first.append(jnp.where(keep, jnp.where(low_half, a, pltpu.roll(b, RIM, axis=1)), 0.0))
            second.append(jnp.where(keep, jnp.where(low_half, pltpu.roll(a, RIM, axis=1), b), 0.0))
        cluster_sums(first, q, 2)
        cluster_sums(second, q + 5, 2)
        return 0

    lax.fori_loop(0, 5, rim_integrals, 0)

    for f in range(NF):
        y[...] = dot(amat[0 : Q * 2 * B, :], gmat[f]).astype(BF16)
        side = nbr_face[f : f + 1, :]

        def project(q, _, f=f, side=side):
            half = y[pl.ds(pl.multiple_of(q * 2 * B, 16), 2 * B), :]
            table = dot(f4b[...], jnp.concatenate([half, half, jnp.zeros((32, E), BF16)], axis=0))
            picked = table[0:24]
            for s in range(1, NF):
                picked = jnp.where(side == s, table[s * GP : s * GP + 24], picked)
            nb[q, f * GP : f * GP + 24, :] = picked
            return 0

        lax.fori_loop(0, Q, project, 0, unroll=True)

    arrive(lo_copy, LO, mp2, rp, 32, 1)
    by_slot = sum(dot(piece, mem[...]) for piece in split3(jnp.transpose(rp[...])))
    by_slot = jnp.where(iota((128, E), 0) == 96, 1.0, by_slot)
    slot_state = by_slot[72:96]
    slot_pieces = split3(by_slot)
    slips = []
    for f in range(NF):
        table = etab[f * E : (f + 1) * E, :]
        grid = sum(dot_nt(piece, table) for piece in slot_pieces)
        rate, stress, imp, var = grid[0:24], grid[24:48], grid[48:72], grid[72:96]
        here = grid[96:97] > 0.5
        imp = jnp.where(imp > 0.0, imp, 1.0)
        rows = slice(f * GP, f * GP + 24)
        inner = [of[p, rows, :] / step for p in (0, 3, 7)]
        outer = [nb[p, rows, :] / step for p in (0, 3, 7)]
        locked = 0.5 * (inner[1] + outer[1]) + imp * (outer[2] - inner[2])
        normal = jnp.maximum(stress - 0.5 * (inner[0] + outer[0]), 1.0)
        strength = normal * rate
        gain = 0.5 * jnp.exp(var)
        slip = jnp.zeros_like(locked)
        for _ in range(NEWTON):
            scaled = gain * slip
            mismatch = imp * slip + strength * inverse_sinh(scaled) - locked
            tangent = imp + strength * gain / jnp.sqrt(1.0 + scaled * scaled)
            slip = slip - mismatch / tangent
        traction = locked - imp * slip
        nb[3, rows, :] = jnp.where(here, step * traction, nb[3, rows, :])
        nb[7, rows, :] = jnp.where(here, step * (inner[2] + slip), nb[7, rows, :])
        slips.append(split3(jnp.where(here, slip, 0.0)))
    slot_slip = jnp.zeros((24, E), F32)
    for f in range(NF):
        for piece in slips[f]:
            slot_slip = slot_slip + dot(piece, etab[f * E : (f + 1) * E, :])
    slip_out[...] = slot_slip[0:FB]
    slip_copy = pltpu.make_async_copy(slip_out, slip_h, out_sem.at[1])
    slip_copy.start()
    next_state = STEADY + (slot_state - STEADY) * jnp.exp(-jnp.abs(slot_slip))
    gap8, gap72 = jnp.zeros((8, E), F32), jnp.zeros((72, E), F32)
    wrapped = jnp.concatenate([next_state, gap8, next_state, gap72], axis=0)
    told = sum(dot_nt(mem[...], piece) for piece in split3(wrapped)).reshape(LO, 2, HI, 128)
    bs[...] = jnp.where(lane3 < 32, told[:, 0], told[:, 1]).reshape(n, 128)
    send(lo_copy, LO, lo, bs, ms, HI, 2)

    in_copies[2].wait()

    def fluxes(g, _):
        for l in range(2):
            lanes = slice(l * 128, (l + 1) * 128)
            for f in range(NF):
                rows = slice(f * GP, f * GP + 24)
                total = [jnp.zeros((24, 128), F32) for _ in range(3)]
                for q in range(Q):
                    mine, other = of[q, rows, lanes], nb[q, rows, lanes]
                    for i in range(3):
                        total[i] = total[i] + flux[0, g * 3 + i, q, f : f + 1, lanes] * mine
                        total[i] = total[i] + flux[1, g * 3 + i, q, f : f + 1, lanes] * other
                for i in range(3):
                    fx[g * 3 + i, rows, lanes] = total[i]
        return 0

    lax.fori_loop(0, 3, fluxes, 0)

    arrive(lo_copy, LO, bs, ms, HI, 2)
    for t in range(HI):
        ms2[t * LO : (t + 1) * LO, :] = ms[pl.ds(t, LO, stride=HI), :]
    send(hi_copy, HI, hi, ms2, rs, LO, 2)

    def lifted(p, _):
        high, low = split2(fx[p])
        both = jnp.concatenate([high, low], axis=0).astype(BF16)
        surface = dot(l2[...], both)
        acc[p] = acc[p] - (surface[0:B] + surface[B : 2 * B])
        return 0

    lax.fori_loop(0, Q, lifted, 0, unroll=True)
    out_copy = pltpu.make_async_copy(acc, out_h, out_sem.at[0])
    out_copy.start()

    arrive(hi_copy, HI, ms2, rs, LO, 2)
    turned = jnp.transpose(rs[...])
    news = jnp.concatenate([turned[0:24], turned[32:56]], axis=1)
    update = sum(dot(piece, own_of[...]) for piece in split3(news))
    hit = dot(jnp.ones((16, E), BF16), own_of[...])[0:1] > 0.5
    state_out[...] = jnp.where(hit, update[0:FB], state[...])
    state_copy = pltpu.make_async_copy(state_out, state_h, out_sem.at[2])
    state_copy.start()

    sent(lo_copy, LO, bq, mq, HI, 0)
    sent(hi_copy, HI, mq2, rq, LO, 0)
    sent(hi_copy, HI, bp, mp, 16, 1)
    sent(lo_copy, LO, mp2, rp, 32, 1)
    sent(lo_copy, LO, bs, ms, HI, 2)
    sent(hi_copy, HI, ms2, rs, LO, 2)
    for k in range(ORD):
        for copy in halo_copies(k):
            copy.wait_send()
    out_copy.wait()
    slip_copy.wait()
    state_copy.wait()


def local(*args):
    (elem_dofs, star_mats, flux_solver, stiffness, face_proj, lift_mats, neighbours, neighbour_face,
     cluster, fault_elem, fault_face, fault_target, fault_params, fault_state) = args
    anywhere = pl.BlockSpec(memory_space=pl.ANY)
    halo = pltpu.VMEM((ORD, 5, B, 128), F32)
    small = pltpu.VMEM((LO * HI, 128), F32)
    double = pltpu.VMEM((2 * LO * HI, 128), F32)
    faces = pltpu.VMEM((Q, NF * GP, E), F32)
    square = pltpu.VMEM((E, E), BF16)
    row = pltpu.VMEM((1, E), I32)
    out, slip, state = pl.pallas_call(
        kernel,
        out_shape=(
            jax.ShapeDtypeStruct((Q, B, E), F32),
            jax.ShapeDtypeStruct((FB, E), F32),
            jax.ShapeDtypeStruct((FB, E), F32),
        ),
        in_specs=[anywhere] * 14,
        out_specs=(anywhere,) * 3,
        scratch_shapes=[
            pltpu.VMEM((3, B, B), F32),
            pltpu.VMEM((FB, NF, B), F32),
            pltpu.VMEM((FB, NF, B), F32),
            pltpu.VMEM((NF, E), I32),
            pltpu.VMEM((NF, E), I32),
            row, row, row, row,
            pltpu.VMEM((3, FB, E), F32),
            pltpu.VMEM((FB, E), F32),
            pltpu.VMEM((FB, E), F32),
            pltpu.VMEM((FB, E), F32),
            pltpu.VMEM((ORD, Q, B, E), F32),
            pltpu.VMEM((Q, Q, 3, E), F32),
            pltpu.VMEM((2, Q, Q, NF, E), F32),
            pltpu.VMEM((Q, 3 * B, E), F32),
            pltpu.VMEM((176, 128), F32),
            pltpu.VMEM((128, 128), F32),
            pltpu.VMEM((176, 256), BF16),
            pltpu.VMEM((176, 256), BF16),
            pltpu.VMEM((128, 256), BF16),
            pltpu.VMEM((128, 256), BF16),
            pltpu.VMEM((112, 256), BF16),
            square,
            square,
            pltpu.VMEM((NF * E, E), BF16),
            halo, halo, halo, halo,
            pltpu.VMEM((10 * 2 * B, NC * EXT), BF16),
            pltpu.VMEM((NF, NC * EXT, E), BF16),
            pltpu.VMEM((Q * 2 * B, E), BF16),
            faces, faces, faces,
            pltpu.VMEM((Q, B, E), F32),
            pltpu.VMEM((128, E), F32),
            small, small, small, small,
            double, double, double, double,
            small, small, small, small,
            pltpu.SemaphoreType.DMA((14,)),
            pltpu.SemaphoreType.DMA((3,)),
            pltpu.SemaphoreType.DMA((2, ORD)),
            pltpu.SemaphoreType.DMA((2, ORD)),
            pltpu.SemaphoreType.DMA((3, LO)),
            pltpu.SemaphoreType.DMA((3, LO)),
            pltpu.SemaphoreType.DMA((3, HI)),
            pltpu.SemaphoreType.DMA((3, HI)),
        ],
        compiler_params=pltpu.CompilerParams(
            collective_id=0, has_side_effects=True, vmem_limit_bytes=60 * 1024 * 1024
        ),
    )(
        jnp.transpose(elem_dofs, (1, 0, 2)),
        jnp.transpose(star_mats, (1, 2, 0, 3)),
        jnp.transpose(flux_solver, (0, 2, 3, 1, 4)),
        stiffness,
        jnp.transpose(face_proj, (1, 0, 2)),
        jnp.transpose(lift_mats, (2, 0, 1)),
        neighbours,
        neighbour_face,
        cluster.reshape(1, E),
        fault_elem.reshape(1, E),
        fault_face.reshape(1, E),
        fault_target.reshape(1, E),
        fault_params,
        fault_state,
    )
    return jnp.transpose(out, (1, 0, 2)), slip, state


def solution(mesh):
    return jax.shard_map(
        local,
        mesh=mesh,
        in_specs=(
            P(None, None, "dom"),
            P(None, None, None, "dom"),
            P(None, None, None, None, "dom"),
            P(),
            P(),
            P(),
            P(None, "dom"),
            P(None, "dom"),
            P("dom"),
            P("dom"),
            P("dom"),
            P("dom"),
            P(None, None, "dom"),
            P(None, "dom"),
        ),
        out_specs=(P(None, None, "dom"), P(None, "dom"), P(None, "dom")),
        check_vma=False,
    )
```

```python
import functools

import jax
import jax.numpy as jnp
from jax import lax
from jax.experimental import pallas as pl
from jax.experimental.pallas import tpu as pltpu
from jax.sharding import PartitionSpec as P

F32, BF16, I32 = jnp.float32, jnp.bfloat16, jnp.int32
MESH = pl.DeviceIdType.MESH
B, Q, FB, ORD, NF, NC, NEWTON = 56, 9, 21, 6, 4, 4, 4
E, RIM = 256, 64
N = 128
ORDER = (0, 3, 7, 1, 2, 4, 5, 6, 8)
FIRST = 3 * 2 * B
GP = 32
EXT = 384
BASE_STEP, STEADY = 0.2, 0.8
TAUS = [BASE_STEP * 2.0**c for c in range(NC)]


def term_weights(tau):
    out, weight = [], 1.0
    for degree in range(ORD):
        weight = weight * tau / (degree + 1)
        out.append(weight)
    return out


WEIGHTS = [term_weights(tau) for tau in TAUS]


def iota(shape, dim):
    return lax.broadcasted_iota(I32, shape, dim)


def dot(a, b):
    return jnp.dot(a, b, preferred_element_type=F32)


def dot_nt(a, b):
    return lax.dot_general(a, b, (((1,), (1,)), ((), ())), preferred_element_type=F32)


def split2(x):
    high = x.astype(BF16).astype(F32)
    return high, x - high


def split3(x):
    high = x.astype(BF16)
    rest = x - high.astype(F32)
    mid = rest.astype(BF16)
    low = (rest - mid.astype(F32)).astype(BF16)
    return high, mid, low


def stacked(x):
    high, low = split2(x)
    gap = jnp.zeros((8, x.shape[1]), F32)
    half = jnp.concatenate([high, gap, low, gap], axis=0).astype(BF16)
    return jnp.concatenate([half, half], axis=0)


def left_factor(w):
    both = w + pltpu.roll(w, 64, axis=1)
    high, low = split2(both)
    return jnp.concatenate([high.astype(BF16), low.astype(BF16)], axis=1)


def inverse_sinh(value):
    magnitude = jnp.abs(value)
    result = jnp.log(magnitude + jnp.sqrt(1.0 + magnitude * magnitude))
    return jnp.where(value < 0.0, -result, result)


def kernel(
    dofs_h, star_h, flux_h, *rest
):
    small_h, rest = rest[:11], rest[11:]
    (acc, slip_out, state_out), rest = rest[:3], rest[3:]
    small_v, rest = rest[:11], rest[11:]
    stiff, proj, lift, nbr, nbr_face, cluster, f_elem, f_face, f_target, params, state = small_v
    (x, star, flux, st, wide, pad_sq, s4, st4, f4, f4b, l2, mem, own_of, etab,
    hsl, hsr, hrl, hrr, amat, gmat, y, of, nb, fx, pp,
    bq, rq, bp, rp, bs, rs,
    in_sem, hs_sem, hr_sem, ex_s, ex_r, ex_o) = rest
    me = lax.axis_index("dom")
    n = N
    left, right = (me + n - 1) % n, (me + 1) % n

    in_copies = [
        pltpu.make_async_copy(dofs_h, x.at[0], in_sem.at[0]),
        pltpu.make_async_copy(star_h, star, in_sem.at[1]),
        pltpu.make_async_copy(flux_h, flux, in_sem.at[2]),
    ]
    small_copies = [
        pltpu.make_async_copy(source, place, in_sem.at[3 + i])
        for i, (source, place) in enumerate(zip(small_h, small_v))
    ]
    for copy in small_copies + in_copies:
        copy.start()

    barrier = pltpu.get_barrier_semaphore()

    def greet(j, _):
        pl.semaphore_signal(barrier, inc=1, device_id=((me + j) % n,), device_id_type=MESH)
        return 0

    lax.fori_loop(1, n, greet, 0)

    def row_copy(buf, dst, rows, which, j):
        t = (me + j) % n
        return pltpu.make_async_remote_copy(
            src_ref=buf.at[pl.ds(t * rows, rows)],
            dst_ref=dst.at[pl.ds(me * rows, rows)],
            send_sem=ex_s.at[which], recv_sem=ex_r.at[which],
            device_id=(t,), device_id_type=MESH,
        )

    def send(buf, dst, rows, which):
        def one(j, _):
            row_copy(buf, dst, rows, which, j).start()
            return 0

        lax.fori_loop(1, n, one, 0)
        pltpu.make_async_copy(buf.at[pl.ds(me * rows, rows)], dst.at[pl.ds(me * rows, rows)], ex_o.at[which]).start()

    def arrive(buf, dst, rows, which):
        pltpu.make_async_copy(buf.at[pl.ds(me * rows, rows)], dst.at[pl.ds(me * rows, rows)], ex_o.at[which]).wait()
        pltpu.make_async_copy(
            buf.at[pl.ds(0, (n - 1) * rows)], dst.at[pl.ds(0, (n - 1) * rows)], ex_r.at[which]
        ).wait()

    def sent(buf, dst, rows, which):
        pltpu.make_async_copy(
            buf.at[pl.ds(0, (n - 1) * rows)], dst.at[pl.ds(0, (n - 1) * rows)], ex_s.at[which]
        ).wait()

    def halo_copies(k):
        return (
            pltpu.make_async_remote_copy(
                src_ref=hsl.at[k], dst_ref=hrr.at[k], send_sem=hs_sem.at[0, k], recv_sem=hr_sem.at[0, k],
                device_id=(left,), device_id_type=MESH),
            pltpu.make_async_remote_copy(
                src_ref=hsr.at[k], dst_ref=hrl.at[k], send_sem=hs_sem.at[1, k], recv_sem=hr_sem.at[1, k],
                device_id=(right,), device_id_type=MESH),
        )

    for copy in small_copies:
        copy.wait()
    wide[...] = jnp.zeros_like(wide)
    for d in range(3):
        wide[d * B : (d + 1) * B, 0:B] = stiff[d]
    s4[...] = left_factor(wide[...])
    for d in range(3):
        pad_sq[...] = jnp.zeros_like(pad_sq)
        pad_sq[0:B, 0:B] = stiff[d]
        wide[d * B : (d + 1) * B, :] = jnp.transpose(pad_sq[...])[0:B]
    st4[...] = left_factor(wide[...])
    pad_sq[...] = jnp.zeros_like(pad_sq)
    for f in range(NF):
        pad_sq[f * GP : f * GP + FB, 0:B] = proj[:, f, :]
    f4[...] = left_factor(pad_sq[...])
    pad_sq[...] = jnp.zeros_like(pad_sq)
    for f in range(NF):
        pad_sq[f * 24 : f * 24 + FB, 0:B] = proj[:, f, :]
    high, low = [jnp.concatenate([v, jnp.zeros((96, 128), F32)], axis=1) for v in split2(pad_sq[0:96, :])]
    f4b[...] = (
        high + pltpu.roll(high, B, axis=1) + pltpu.roll(low, 2 * B, axis=1) + pltpu.roll(low, 3 * B, axis=1)
    ).astype(BF16)
    pad_sq[...] = jnp.zeros_like(pad_sq)
    for f in range(NF):
        pad_sq[f * GP : f * GP + FB, 0:B] = lift[:, f, :]
    lift_high, lift_low = split2(jnp.transpose(pad_sq[...])[0:B])
    lift_rows = jnp.concatenate([lift_high, lift_low], axis=0).astype(BF16)
    l2[...] = jnp.concatenate([lift_rows, lift_rows], axis=1)
    fx[...] = jnp.zeros_like(fx)
    pp[...] = jnp.zeros_like(pp)
    for j in range(3):
        pp[24 * j : 24 * j + FB, :] = params[j]
    pp[72 : 72 + FB, :] = state[...]

    target = f_target[...]
    live = target >= 0
    owner = jnp.where(live, lax.shift_right_logical(target, 8), -1)
    slot = jnp.bitwise_and(target, E - 1)
    member = jnp.where(iota((n, E), 0) == owner, 1.0, 0.0)
    earlier = jnp.where(iota((E, E), 0) < iota((E, E), 1), 1.0, 0.0).astype(BF16)
    before = dot(member.astype(BF16), earlier)
    rank = jnp.sum(member * before, axis=0, keepdims=True)
    place = owner.astype(F32) + n * rank
    place = jnp.where(live, place, -1.0)
    mem[...] = jnp.where(iota((E, E), 0).astype(F32) == place, 1.0, 0.0).astype(BF16)
    grid_place = jnp.where(live, f_face[...] * E + f_elem[...], -1)
    for f in range(NF):
        etab[f * E : (f + 1) * E, :] = jnp.where(iota((E, E), 0) + f * E == grid_place, 1.0, 0.0).astype(BF16)
    ids = jnp.where(iota((128, E), 0) < 2, (slot + 1).astype(F32), 0.0).astype(BF16)
    asked = dot_nt(mem[...], ids)
    lane2 = iota((n, 128), 1)
    bq[...] = jnp.where(lane2 == 0, asked[0:n], asked[n : 2 * n])

    lane = iota((B, 128), 1)
    low_half = lane < RIM

    def pack_halo(k):
        for q in range(5):
            r = min(q + 5, Q - 1)
            hsl[k, q] = jnp.where(low_half, x[k, q, :, 0:128], pltpu.roll(x[k, r, :, 0:128], RIM, axis=1))
            hsr[k, q] = jnp.where(low_half, pltpu.roll(x[k, q, :, 128:256], RIM, axis=1), x[k, r, :, 128:256])
        for copy in halo_copies(k):
            copy.start()

    def star_products(left_w, source):
        def one(q, _):
            st[q] = dot(left_w[...], stacked(source(q)))[0 : 3 * B]
            return 0

        lax.fori_loop(0, Q, one, 0, unroll=True)

    def star_sum(store):
        def one(g, _):
            for l in range(2):
                lanes = slice(l * 128, (l + 1) * 128)
                total = [jnp.zeros((B, 128), F32) for _ in range(3)]
                for q in range(Q):
                    for d in range(3):
                        value = st[q, d * B : (d + 1) * B, lanes]
                        for i in range(3):
                            total[i] = total[i] + star[g * 3 + i, q, d : d + 1, lanes] * value
                for i in range(3):
                    store(g * 3 + i, lanes, total[i])
            return 0

        lax.fori_loop(0, 3, one, 0)

    def taylor(k):
        star_products(s4, lambda q: x[k - 1, q])

        def store(p, lanes, value):
            x[k, p, :, lanes] = value

        star_sum(store)

    for copy in in_copies[:2]:
        copy.wait()
    taylor(1)
    pl.semaphore_wait(barrier, n - 1)
    pack_halo(0)
    pack_halo(1)
    send(bq, rq, 1, 0)
    for k in range(2, ORD):
        taylor(k)
        pack_halo(k)

    arrive(bq, rq, 1, 0)
    wanted = (iota((n, E), 1) + 1).astype(F32)
    for r in range(2):
        own_of[r * n : (r + 1) * n, :] = jnp.where(rq[:, r : r + 1] == wanted, 1.0, 0.0).astype(BF16)
    answer = sum(dot_nt(own_of[...], piece) for piece in split3(pp[...]))
    for r in range(2):
        bp[pl.ds(r, n, stride=2), :] = answer[r * n : (r + 1) * n]
    send(bp, rp, 2, 1)

    level = cluster[...]

    def by_level(values):
        out = jnp.full((1, E), values[0], F32)
        for c in range(1, NC):
            out = jnp.where(level == c, values[c], out)
        return out

    step = by_level(TAUS)
    own_w = [by_level([WEIGHTS[c][k] for c in range(NC)]) for k in range(ORD)]

    def own_term(q, _):
        total = own_w[0] * x[0, q]
        for k in range(1, ORD):
            total = total + own_w[k] * x[k, q]
        wrapped = stacked(total)
        st[q] = dot(st4[...], wrapped)[0 : 3 * B]
        of[q] = dot(f4[...], wrapped)
        return 0

    lax.fori_loop(0, Q, own_term, 0, unroll=3)

    number = nbr[...] - me * E
    ext = jnp.where(number < RIM, number + E, jnp.where(number >= E + RIM, number, number - RIM))
    column = level * EXT + ext
    for f in range(NF):
        def build(c, _, f=f):
            rows = pl.ds(pl.multiple_of(c * E, E), E)
            hit = iota((E, E), 0) + c * E == column[f : f + 1]
            gmat[f, rows, :] = jnp.where(hit, 1.0, 0.0).astype(BF16)
            return 0

        lax.fori_loop(0, NC * EXT // E, build, 0)

    def cluster_sums(terms, row, l):
        for c in range(NC):
            total = WEIGHTS[c][0] * terms[0]
            for k in range(1, ORD):
                total = total + WEIGHTS[c][k] * terms[k]
            high, low = split2(total)
            rows = slice(row * 2 * B, (row + 1) * 2 * B)
            lanes = slice(c * EXT + l * 128, c * EXT + (l + 1) * 128)
            amat[rows, lanes] = jnp.concatenate([high, low], axis=0).astype(BF16)

    for q in range(Q):
        for l in range(2):
            cluster_sums([x[k, q, :, l * 128 : (l + 1) * 128] for k in range(ORD)], ORDER.index(q), l)

    keep_low = jnp.where(me > 0, 1, 0)
    keep_high = jnp.where(me < n - 1, 1, 0)
    keep = jnp.where(lane < RIM, keep_low, keep_high) > 0
    for k in range(ORD):
        for copy in halo_copies(k):
            copy.wait_recv()

    for q in range(5):
        first, second = [], []
        for k in range(ORD):
            a, b = hrl[k, q], hrr[k, q]
            first.append(jnp.where(keep, jnp.where(low_half, a, pltpu.roll(b, RIM, axis=1)), 0.0))
            if q + 5 < Q:
                second.append(jnp.where(keep, jnp.where(low_half, pltpu.roll(a, RIM, axis=1), b), 0.0))
        cluster_sums(first, ORDER.index(q), 2)
        if q + 5 < Q:
            cluster_sums(second, ORDER.index(q + 5), 2)

    def gather(start, stop):
        def one(f, _):
            y[f, start:stop, :] = dot(amat[start:stop, :], gmat[f]).astype(BF16)
            return 0

        lax.fori_loop(0, NF, one, 0)

    def project(q):
        start = ORDER.index(q) * 2 * B
        for f in range(NF):
            side = nbr_face[f : f + 1, :]
            half = y[f, start : start + 2 * B, :]
            table = dot(f4b[...], jnp.concatenate([half, half, jnp.zeros((32, E), BF16)], axis=0))
            picked = table[0:24]
            for s in range(1, NF):
                picked = jnp.where(side == s, table[s * 24 : (s + 1) * 24], picked)
            nb[q, f * GP : f * GP + 24, :] = picked

    gather(0, FIRST)
    for q in ORDER[:3]:
        project(q)

    arrive(bp, rp, 2, 1)
    given = jnp.concatenate([rp[pl.ds(r, n, stride=2), :] for r in range(2)], axis=0)
    by_slot = sum(dot(piece, mem[...]) for piece in split3(jnp.transpose(given)))
    by_slot = jnp.where(iota((128, E), 0) == 96, 1.0, by_slot)
    slot_state = by_slot[72:96]
    slot_pieces = split3(by_slot)
    slips = []
    for f in range(NF):
        table = etab[f * E : (f + 1) * E, :]
        grid = sum(dot_nt(piece, table) for piece in slot_pieces)
        rate, stress, imp, var = grid[0:24], grid[24:48], grid[48:72], grid[72:96]
        here = grid[96:97] > 0.5
        imp = jnp.where(imp > 0.0, imp, 1.0)
        rows = slice(f * GP, f * GP + 24)
        inner = [of[p, rows, :] / step for p in (0, 3, 7)]
        outer = [nb[p, rows, :] / step for p in (0, 3, 7)]
        locked = 0.5 * (inner[1] + outer[1]) + imp * (outer[2] - inner[2])
        normal = jnp.maximum(stress - 0.5 * (inner[0] + outer[0]), 1.0)
        strength = normal * rate
        gain = 0.5 * jnp.exp(var)
        slip = jnp.zeros_like(locked)
        for _ in range(NEWTON):
            scaled = gain * slip
            mismatch = imp * slip + strength * inverse_sinh(scaled) - locked
            tangent = imp + strength * gain / jnp.sqrt(1.0 + scaled * scaled)
            slip = slip - mismatch / tangent
        traction = locked - imp * slip
        nb[3, rows, :] = jnp.where(here, step * traction, nb[3, rows, :])
        nb[7, rows, :] = jnp.where(here, step * (inner[2] + slip), nb[7, rows, :])
        slips.append(split3(jnp.where(here, slip, 0.0)))
    slot_slip = jnp.zeros((24, E), F32)
    for f in range(NF):
        for piece in slips[f]:
            slot_slip = slot_slip + dot(piece, etab[f * E : (f + 1) * E, :])
    slip_out[...] = slot_slip[0:FB]
    next_state = STEADY + (slot_state - STEADY) * jnp.exp(-jnp.abs(slot_slip))
    gap8, gap72 = jnp.zeros((8, E), F32), jnp.zeros((72, E), F32)
    wrapped = jnp.concatenate([next_state, gap8, next_state, gap72], axis=0)
    told = sum(dot_nt(mem[...], piece) for piece in split3(wrapped))
    bs[...] = jnp.where(lane2 < 32, told[0:n], told[n : 2 * n])
    send(bs, rs, 1, 2)

    gather(FIRST, Q * 2 * B)
    for q in ORDER[3:]:
        project(q)

    def store_volume(p, lanes, value):
        acc[p, :, lanes] = x[0, p, :, lanes] + value

    star_sum(store_volume)

    in_copies[2].wait()

    def fluxes(g, _):
        for l in range(2):
            lanes = slice(l * 128, (l + 1) * 128)
            for f in range(NF):
                rows = slice(f * GP, f * GP + 24)
                total = [jnp.zeros((24, 128), F32) for _ in range(3)]
                for q in range(Q):
                    mine, other = of[q, rows, lanes], nb[q, rows, lanes]
                    for i in range(3):
                        total[i] = total[i] + flux[0, g * 3 + i, q, f : f + 1, lanes] * mine
                        total[i] = total[i] + flux[1, g * 3 + i, q, f : f + 1, lanes] * other
                for i in range(3):
                    fx[g * 3 + i, rows, lanes] = total[i]
        return 0

    lax.fori_loop(0, 3, fluxes, 0)

    def lifted(p, _):
        high, low = split2(fx[p])
        both = jnp.concatenate([high, low], axis=0).astype(BF16)
        surface = dot(l2[...], both)
        acc[p] = acc[p] - (surface[0:B] + surface[B : 2 * B])
        return 0

    lax.fori_loop(0, Q, lifted, 0, unroll=True)
    arrive(bs, rs, 1, 2)
    turned = jnp.transpose(rs[...])
    news = jnp.concatenate([turned[0:24], turned[32:56]], axis=1)
    update = sum(dot(piece, own_of[...]) for piece in split3(news))
    hit = dot(jnp.ones((16, E), BF16), own_of[...])[0:1] > 0.5
    state_out[...] = jnp.where(hit, update[0:FB], state[...])

    sent(bq, rq, 1, 0)
    sent(bp, rp, 2, 1)
    sent(bs, rs, 1, 2)
    for k in range(ORD):
        for copy in halo_copies(k):
            copy.wait_send()


def local(*args):
    (elem_dofs, star_mats, flux_solver, stiffness, face_proj, lift_mats, neighbours, neighbour_face,
     cluster, fault_elem, fault_face, fault_target, fault_params, fault_state) = args
    vmem, hbm = pl.BlockSpec(memory_space=pltpu.VMEM), pl.BlockSpec(memory_space=pl.ANY)
    halo = pltpu.VMEM((ORD, 5, B, 128), F32)
    small = pltpu.VMEM((N, 128), F32)
    double = pltpu.VMEM((2 * N, 128), F32)
    faces = pltpu.VMEM((Q, NF * GP, E), F32)
    square = pltpu.VMEM((E, E), BF16)
    row = pltpu.VMEM((1, E), I32)
    out, slip, state = pl.pallas_call(
        kernel,
        out_shape=(
            jax.ShapeDtypeStruct((Q, B, E), F32),
            jax.ShapeDtypeStruct((FB, E), F32),
            jax.ShapeDtypeStruct((FB, E), F32),
        ),
        in_specs=[hbm] * 14,
        out_specs=(vmem,) * 3,
        scratch_shapes=[
            pltpu.VMEM((3, B, B), F32),
            pltpu.VMEM((FB, NF, B), F32),
            pltpu.VMEM((FB, NF, B), F32),
            pltpu.VMEM((NF, E), I32),
            pltpu.VMEM((NF, E), I32),
            row, row, row, row,
            pltpu.VMEM((3, FB, E), F32),
            pltpu.VMEM((FB, E), F32),
            pltpu.VMEM((ORD, Q, B, E), F32),
            pltpu.VMEM((Q, Q, 3, E), F32),
            pltpu.VMEM((2, Q, Q, NF, E), F32),
            pltpu.VMEM((Q, 3 * B, E), F32),
            pltpu.VMEM((176, 128), F32),
            pltpu.VMEM((128, 128), F32),
            pltpu.VMEM((176, 256), BF16),
            pltpu.VMEM((176, 256), BF16),
            pltpu.VMEM((128, 256), BF16),
            pltpu.VMEM((96, 256), BF16),
            pltpu.VMEM((112, 256), BF16),
            square,
            square,
            pltpu.VMEM((NF * E, E), BF16),
            halo, halo, halo, halo,
            pltpu.VMEM((Q * 2 * B, NC * EXT), BF16),
            pltpu.VMEM((NF, NC * EXT, E), BF16),
            pltpu.VMEM((NF, Q * 2 * B, E), BF16),
            faces, faces, faces,
            pltpu.VMEM((128, E), F32),
            small, small, double, double, small, small,
            pltpu.SemaphoreType.DMA((14,)),
            pltpu.SemaphoreType.DMA((2, ORD)),
            pltpu.SemaphoreType.DMA((2, ORD)),
            pltpu.SemaphoreType.DMA((3,)),
            pltpu.SemaphoreType.DMA((3,)),
            pltpu.SemaphoreType.DMA((3,)),
        ],
        compiler_params=pltpu.CompilerParams(
            collective_id=0, has_side_effects=True, vmem_limit_bytes=60 * 1024 * 1024
        ),
    )(
        jnp.transpose(elem_dofs, (1, 0, 2)),
        jnp.transpose(star_mats, (1, 2, 0, 3)),
        jnp.transpose(flux_solver, (0, 2, 3, 1, 4)),
        stiffness,
        jnp.transpose(face_proj, (1, 0, 2)),
        jnp.transpose(lift_mats, (2, 0, 1)),
        neighbours,
        neighbour_face,
        cluster.reshape(1, E),
        fault_elem.reshape(1, E),
        fault_face.reshape(1, E),
        fault_target.reshape(1, E),
        fault_params,
        fault_state,
    )
    return jnp.transpose(out, (1, 0, 2)), slip, state


def solution(mesh):
    return jax.shard_map(
        local,
        mesh=mesh,
        in_specs=(
            P(None, None, "dom"),
            P(None, None, None, "dom"),
            P(None, None, None, None, "dom"),
            P(),
            P(),
            P(),
            P(None, "dom"),
            P(None, "dom"),
            P("dom"),
            P("dom"),
            P("dom"),
            P("dom"),
            P(None, None, "dom"),
            P(None, "dom"),
        ),
        out_specs=(P(None, None, "dom"), P(None, "dom"), P(None, "dom")),
        check_vma=False,
    )
```

```python
import functools

import jax
import jax.numpy as jnp
from jax import lax
from jax.experimental import pallas as pl
from jax.experimental.pallas import tpu as pltpu
from jax.sharding import PartitionSpec as P

F32, BF16, I32 = jnp.float32, jnp.bfloat16, jnp.int32
MESH = pl.DeviceIdType.MESH
B, Q, FB, ORD, NF, NC, NEWTON = 56, 9, 21, 6, 4, 4, 4
E, RIM = 256, 64
N = 128
ORDER = (0, 3, 7, 1, 2, 4, 5, 6, 8)
FIRST = 3 * 2 * B
GP = 32
EXT = 384
BASE_STEP, STEADY = 0.2, 0.8
TAUS = [BASE_STEP * 2.0**c for c in range(NC)]


def term_weights(tau):
    out, weight = [], 1.0
    for degree in range(ORD):
        weight = weight * tau / (degree + 1)
        out.append(weight)
    return out


WEIGHTS = [term_weights(tau) for tau in TAUS]


def iota(shape, dim):
    return lax.broadcasted_iota(I32, shape, dim)


def dot(a, b):
    return jnp.dot(a, b, preferred_element_type=F32)


def dot_nt(a, b):
    return lax.dot_general(a, b, (((1,), (1,)), ((), ())), preferred_element_type=F32)


def split2(x):
    high = x.astype(BF16).astype(F32)
    return high, x - high


def split3(x):
    high = x.astype(BF16)
    rest = x - high.astype(F32)
    mid = rest.astype(BF16)
    low = (rest - mid.astype(F32)).astype(BF16)
    return high, mid, low


def stacked(x):
    high, low = split2(x)
    gap = jnp.zeros((8, x.shape[1]), F32)
    half = jnp.concatenate([high, gap, low, gap], axis=0).astype(BF16)
    return jnp.concatenate([half, half], axis=0)


def left_factor(w):
    both = w + pltpu.roll(w, 64, axis=1)
    high, low = split2(both)
    return jnp.concatenate([high.astype(BF16), low.astype(BF16)], axis=1)


def inverse_sinh(value):
    magnitude = jnp.abs(value)
    result = jnp.log(magnitude + jnp.sqrt(1.0 + magnitude * magnitude))
    return jnp.where(value < 0.0, -result, result)


def kernel(
    dofs_h, star_h, flux_h, *rest
):
    small_h, rest = rest[:11], rest[11:]
    (acc, slip_out, state_out), rest = rest[:3], rest[3:]
    small_v, rest = rest[:11], rest[11:]
    stiff, proj, lift, nbr, nbr_face, cluster, f_elem, f_face, f_target, params, state = small_v
    (x, star, flux, st, wide, pad_sq, s4, st4, f4, f4b, l2, mem, own_of, etab,
    hsl, hsr, hrl, hrr, amat, gmat, y, of, nb, fx, pp,
    bq, rq, bp, rp, bs, rs,
    in_sem, hs_sem, hr_sem, ex_s, ex_r, ex_o) = rest
    me = lax.axis_index("dom")
    n = N
    left, right = (me + n - 1) % n, (me + 1) % n

    in_copies = [
        pltpu.make_async_copy(dofs_h, x.at[0], in_sem.at[0]),
        pltpu.make_async_copy(star_h, star, in_sem.at[1]),
        pltpu.make_async_copy(flux_h, flux, in_sem.at[2]),
    ]
    small_copies = [
        pltpu.make_async_copy(source, place, in_sem.at[3 + i])
        for i, (source, place) in enumerate(zip(small_h, small_v))
    ]
    for copy in small_copies + in_copies:
        copy.start()

    barrier = pltpu.get_barrier_semaphore()

    def others(action):
        def one(t, _):
            action(t)
            return 0

        lax.fori_loop(me + 1, n, one, 0)
        lax.fori_loop(0, me, one, 0)

    others(lambda t: pl.semaphore_signal(barrier, inc=1, device_id=(t,), device_id_type=MESH))

    def row_copy(buf, dst, rows, which, t):
        return pltpu.make_async_remote_copy(
            src_ref=buf.at[pl.ds(t * rows, rows)],
            dst_ref=dst.at[pl.ds(me * rows, rows)],
            send_sem=ex_s.at[which], recv_sem=ex_r.at[which],
            device_id=(t,), device_id_type=MESH,
        )

    def send(buf, dst, rows, which):
        others(lambda t: row_copy(buf, dst, rows, which, t).start())
        pltpu.make_async_copy(buf.at[pl.ds(me * rows, rows)], dst.at[pl.ds(me * rows, rows)], ex_o.at[which]).start()

    def arrive(buf, dst, rows, which):
        pltpu.make_async_copy(buf.at[pl.ds(me * rows, rows)], dst.at[pl.ds(me * rows, rows)], ex_o.at[which]).wait()
        pltpu.make_async_copy(
            buf.at[pl.ds(0, (n - 1) * rows)], dst.at[pl.ds(0, (n - 1) * rows)], ex_r.at[which]
        ).wait()

    def sent(buf, dst, rows, which):
        pltpu.make_async_copy(
            buf.at[pl.ds(0, (n - 1) * rows)], dst.at[pl.ds(0, (n - 1) * rows)], ex_s.at[which]
        ).wait()

    def halo_copies(k):
        return (
            pltpu.make_async_remote_copy(
                src_ref=hsl.at[k], dst_ref=hrr.at[k], send_sem=hs_sem.at[0, k], recv_sem=hr_sem.at[0, k],
                device_id=(left,), device_id_type=MESH),
            pltpu.make_async_remote_copy(
                src_ref=hsr.at[k], dst_ref=hrl.at[k], send_sem=hs_sem.at[1, k], recv_sem=hr_sem.at[1, k],
                device_id=(right,), device_id_type=MESH),
        )

    for copy in small_copies:
        copy.wait()
    wide[...] = jnp.zeros_like(wide)
    for d in range(3):
        wide[d * B : (d + 1) * B, 0:B] = stiff[d]
    s4[...] = left_factor(wide[...])
    for d in range(3):
        pad_sq[...] = jnp.zeros_like(pad_sq)
        pad_sq[0:B, 0:B] = stiff[d]
        wide[d * B : (d + 1) * B, :] = jnp.transpose(pad_sq[...])[0:B]
    st4[...] = left_factor(wide[...])
    pad_sq[...] = jnp.zeros_like(pad_sq)
    for f in range(NF):
        pad_sq[f * GP : f * GP + FB, 0:B] = proj[:, f, :]
    f4[...] = left_factor(pad_sq[...])
    pad_sq[...] = jnp.zeros_like(pad_sq)
    for f in range(NF):
        pad_sq[f * 24 : f * 24 + FB, 0:B] = proj[:, f, :]
    high, low = [jnp.concatenate([v, jnp.zeros((96, 128), F32)], axis=1) for v in split2(pad_sq[0:96, :])]
    f4b[...] = (
        high + pltpu.roll(high, B, axis=1) + pltpu.roll(low, 2 * B, axis=1) + pltpu.roll(low, 3 * B, axis=1)
    ).astype(BF16)
    pad_sq[...] = jnp.zeros_like(pad_sq)
    for f in range(NF):
        pad_sq[f * GP : f * GP + FB, 0:B] = lift[:, f, :]
    lift_high, lift_low = split2(jnp.transpose(pad_sq[...])[0:B])
    lift_rows = jnp.concatenate([lift_high, lift_low], axis=0).astype(BF16)
    l2[...] = jnp.concatenate([lift_rows, lift_rows], axis=1)
    fx[...] = jnp.zeros_like(fx)
    pp[...] = jnp.zeros_like(pp)
    for j in range(3):
        pp[24 * j : 24 * j + FB, :] = params[j]
    pp[72 : 72 + FB, :] = state[...]

    target = f_target[...]
    live = target >= 0
    owner = jnp.where(live, lax.shift_right_logical(target, 8), -1)
    slot = jnp.bitwise_and(target, E - 1)
    member = jnp.where(iota((n, E), 0) == owner, 1.0, 0.0)
    earlier = jnp.where(iota((E, E), 0) < iota((E, E), 1), 1.0, 0.0).astype(BF16)
    before = dot(member.astype(BF16), earlier)
    rank = jnp.sum(member * before, axis=0, keepdims=True)
    place = owner.astype(F32) + n * rank
    place = jnp.where(live, place, -1.0)
    mem[...] = jnp.where(iota((E, E), 0).astype(F32) == place, 1.0, 0.0).astype(BF16)
    grid_place = jnp.where(live, f_face[...] * E + f_elem[...], -1)
    for f in range(NF):
        etab[f * E : (f + 1) * E, :] = jnp.where(iota((E, E), 0) + f * E == grid_place, 1.0, 0.0).astype(BF16)
    ids = jnp.where(iota((128, E), 0) < 2, (slot + 1).astype(F32), 0.0).astype(BF16)
    asked = dot_nt(mem[...], ids)
    lane2 = iota((n, 128), 1)
    bq[...] = jnp.where(lane2 == 0, asked[0:n], asked[n : 2 * n])

    lane = iota((32, 128), 1)
    low_half = lane < RIM

    def pack_halo(k, q, half, value):
        if half == 0:
            hsl[k, q] = jnp.where(low_half, value[0:32], pltpu.roll(value[24:56], RIM, axis=1))
        else:
            hsr[k, q] = jnp.where(low_half, pltpu.roll(value[0:32], RIM, axis=1), value[24:56])

    def send_halo(k):
        for copy in halo_copies(k):
            copy.start()

    def star_products(left_w, source):
        def one(q, _):
            st[q] = dot(left_w[...], stacked(source(q)))[0 : 3 * B]
            return 0

        lax.fori_loop(0, Q, one, 0, unroll=True)

    def star_sum(store):
        def one(g, _):
            for l in range(2):
                lanes = slice(l * 128, (l + 1) * 128)
                total = [jnp.zeros((B, 128), F32) for _ in range(3)]
                for q in range(Q):
                    for d in range(3):
                        value = st[q, d * B : (d + 1) * B, lanes]
                        for i in range(3):
                            total[i] = total[i] + star[g * 3 + i, q, d : d + 1, lanes] * value
                for i in range(3):
                    store(g * 3 + i, l, lanes, total[i])
            return 0

        lax.fori_loop(0, 3, one, 0)

    def taylor(k):
        star_products(s4, lambda q: x[k - 1, q])

        def store(p, l, lanes, value):
            x[k, p, :, lanes] = value
            pack_halo(k, p, l, value)

        star_sum(store)

    for copy in in_copies[:2]:
        copy.wait()
    for q in range(Q):
        for l in range(2):
            pack_halo(0, q, l, x[0, q, :, l * 128 : (l + 1) * 128])
    taylor(1)
    pl.semaphore_wait(barrier, n - 1)
    send_halo(0)
    send(bq, rq, 1, 0)
    send_halo(1)
    for k in range(2, ORD - 1):
        taylor(k)
        send_halo(k)

    taylor(ORD - 1)
    send_halo(ORD - 1)

    level = cluster[...]

    def by_level(values):
        out = jnp.full((1, E), values[0], F32)
        for c in range(1, NC):
            out = jnp.where(level == c, values[c], out)
        return out

    step = by_level(TAUS)
    own_w = [by_level([WEIGHTS[c][k] for c in range(NC)]) for k in range(ORD)]

    def own_term(q, _):
        total = own_w[0] * x[0, q]
        for k in range(1, ORD):
            total = total + own_w[k] * x[k, q]
        wrapped = stacked(total)
        st[q] = dot(st4[...], wrapped)[0 : 3 * B]
        of[q] = dot(f4[...], wrapped)
        return 0

    lax.fori_loop(0, Q, own_term, 0, unroll=3)

    arrive(bq, rq, 1, 0)
    wanted = (iota((n, E), 1) + 1).astype(F32)
    for r in range(2):
        own_of[r * n : (r + 1) * n, :] = jnp.where(rq[:, r : r + 1] == wanted, 1.0, 0.0).astype(BF16)
    answer = sum(dot_nt(own_of[...], piece) for piece in split3(pp[...]))
    for r in range(2):
        bp[pl.ds(r, n, stride=2), :] = answer[r * n : (r + 1) * n]
    send(bp, rp, 2, 1)
    number = nbr[...] - me * E
    ext = jnp.where(number < RIM, number + E, jnp.where(number >= E + RIM, number, number - RIM))
    column = level * EXT + ext
    for f in range(NF):
        def build(c, _, f=f):
            rows = pl.ds(pl.multiple_of(c * E, E), E)
            hit = iota((E, E), 0) + c * E == column[f : f + 1]
            gmat[f, rows, :] = jnp.where(hit, 1.0, 0.0).astype(BF16)
            return 0

        lax.fori_loop(0, NC * EXT // E, build, 0)

    def cluster_sums(terms, row, l):
        for c in range(NC):
            total = WEIGHTS[c][0] * terms[0]
            for k in range(1, ORD):
                total = total + WEIGHTS[c][k] * terms[k]
            high, low = split2(total)
            rows = slice(row * 2 * B, (row + 1) * 2 * B)
            lanes = slice(c * EXT + l * 128, c * EXT + (l + 1) * 128)
            amat[rows, lanes] = jnp.concatenate([high, low], axis=0).astype(BF16)

    for q in range(Q):
        for l in range(2):
            cluster_sums([x[k, q, :, l * 128 : (l + 1) * 128] for k in range(ORD)], ORDER.index(q), l)

    keep_low = jnp.where(me > 0, 1, 0)
    keep_high = jnp.where(me < n - 1, 1, 0)
    keep = jnp.where(lane < RIM, keep_low, keep_high) > 0
    for k in range(ORD):
        for copy in halo_copies(k):
            copy.wait_recv()

    for q in range(Q):
        terms = []
        for k in range(ORD):
            a, b = hrl[k, q], hrr[k, q]
            top = jnp.where(keep, jnp.where(low_half, a, pltpu.roll(b, RIM, axis=1)), 0.0)
            bottom = jnp.where(keep, jnp.where(low_half, pltpu.roll(a, RIM, axis=1), b), 0.0)
            terms.append(jnp.concatenate([top, bottom[8:32]], axis=0))
        cluster_sums(terms, ORDER.index(q), 2)

    def gather(start, stop):
        def one(f, _):
            y[f, start:stop, :] = dot(amat[start:stop, :], gmat[f]).astype(BF16)
            return 0

        lax.fori_loop(0, NF, one, 0)

    def project(q):
        start = ORDER.index(q) * 2 * B
        for f in range(NF):
            side = nbr_face[f : f + 1, :]
            half = y[f, start : start + 2 * B, :]
            table = dot(f4b[...], jnp.concatenate([half, half, jnp.zeros((32, E), BF16)], axis=0))
            picked = table[0:24]
            for s in range(1, NF):
                picked = jnp.where(side == s, table[s * 24 : (s + 1) * 24], picked)
            nb[q, f * GP : f * GP + 24, :] = picked

    gather(0, FIRST)
    for q in ORDER[:3]:
        project(q)

    arrive(bp, rp, 2, 1)
    given = jnp.concatenate([rp[pl.ds(r, n, stride=2), :] for r in range(2)], axis=0)
    by_slot = sum(dot(piece, mem[...]) for piece in split3(jnp.transpose(given)))
    by_slot = jnp.where(iota((128, E), 0) == 96, 1.0, by_slot)
    slot_state = by_slot[72:96]
    slot_pieces = split3(by_slot)
    slips = []
    for f in range(NF):
        table = etab[f * E : (f + 1) * E, :]
        grid = sum(dot_nt(piece, table) for piece in slot_pieces)
        rate, stress, imp, var = grid[0:24], grid[24:48], grid[48:72], grid[72:96]
        here = grid[96:97] > 0.5
        imp = jnp.where(imp > 0.0, imp, 1.0)
        rows = slice(f * GP, f * GP + 24)
        inner = [of[p, rows, :] / step for p in (0, 3, 7)]
        outer = [nb[p, rows, :] / step for p in (0, 3, 7)]
        locked = 0.5 * (inner[1] + outer[1]) + imp * (outer[2] - inner[2])
        normal = jnp.maximum(stress - 0.5 * (inner[0] + outer[0]), 1.0)
        strength = normal * rate
        gain = 0.5 * jnp.exp(var)
        slip = jnp.zeros_like(locked)
        for _ in range(NEWTON):
            scaled = gain * slip
            mismatch = imp * slip + strength * inverse_sinh(scaled) - locked
            tangent = imp + strength * gain / jnp.sqrt(1.0 + scaled * scaled)
            slip = slip - mismatch / tangent
        traction = locked - imp * slip
        nb[3, rows, :] = jnp.where(here, step * traction, nb[3, rows, :])
        nb[7, rows, :] = jnp.where(here, step * (inner[2] + slip), nb[7, rows, :])
        slips.append(split3(jnp.where(here, slip, 0.0)))
    slot_slip = jnp.zeros((24, E), F32)
    for f in range(NF):
        for piece in slips[f]:
            slot_slip = slot_slip + dot(piece, etab[f * E : (f + 1) * E, :])
    slip_out[...] = slot_slip[0:FB]
    next_state = STEADY + (slot_state - STEADY) * jnp.exp(-jnp.abs(slot_slip))
    gap8, gap72 = jnp.zeros((8, E), F32), jnp.zeros((72, E), F32)
    wrapped = jnp.concatenate([next_state, gap8, next_state, gap72], axis=0)
    told = sum(dot_nt(mem[...], piece) for piece in split3(wrapped))
    bs[...] = jnp.where(lane2 < 32, told[0:n], told[n : 2 * n])
    send(bs, rs, 1, 2)

    gather(FIRST, Q * 2 * B)
    for q in ORDER[3:]:
        project(q)

    def store_volume(p, _, lanes, value):
        acc[p, :, lanes] = x[0, p, :, lanes] + value

    star_sum(store_volume)

    in_copies[2].wait()

    def fluxes(g, _):
        for l in range(2):
            lanes = slice(l * 128, (l + 1) * 128)
            for f in range(NF):
                rows = slice(f * GP, f * GP + 24)
                total = [jnp.zeros((24, 128), F32) for _ in range(3)]
                for q in range(Q):
                    mine, other = of[q, rows, lanes], nb[q, rows, lanes]
                    for i in range(3):
                        total[i] = total[i] + flux[0, g * 3 + i, q, f : f + 1, lanes] * mine
                        total[i] = total[i] + flux[1, g * 3 + i, q, f : f + 1, lanes] * other
                for i in range(3):
                    fx[g * 3 + i, rows, lanes] = total[i]
        return 0

    lax.fori_loop(0, 3, fluxes, 0)

    def lifted(p, _):
        high, low = split2(fx[p])
        both = jnp.concatenate([high, low], axis=0).astype(BF16)
        surface = dot(l2[...], both)
        acc[p] = acc[p] - (surface[0:B] + surface[B : 2 * B])
        return 0

    lax.fori_loop(0, Q, lifted, 0, unroll=True)
    arrive(bs, rs, 1, 2)
    turned = jnp.transpose(rs[...])
    news = jnp.concatenate([turned[0:24], turned[32:56]], axis=1)
    update = sum(dot(piece, own_of[...]) for piece in split3(news))
    hit = dot(jnp.ones((16, E), BF16), own_of[...])[0:1] > 0.5
    state_out[...] = jnp.where(hit, update[0:FB], state[...])

    sent(bq, rq, 1, 0)
    sent(bp, rp, 2, 1)
    sent(bs, rs, 1, 2)
    for k in range(ORD):
        for copy in halo_copies(k):
            copy.wait_send()


def local(*args):
    (elem_dofs, star_mats, flux_solver, stiffness, face_proj, lift_mats, neighbours, neighbour_face,
     cluster, fault_elem, fault_face, fault_target, fault_params, fault_state) = args
    vmem, hbm = pl.BlockSpec(memory_space=pltpu.VMEM), pl.BlockSpec(memory_space=pltpu.HBM)
    halo = pltpu.VMEM((ORD, Q, 32, 128), F32)
    small = pltpu.VMEM((N, 128), F32)
    double = pltpu.VMEM((2 * N, 128), F32)
    faces = pltpu.VMEM((Q, NF * GP, E), F32)
    square = pltpu.VMEM((E, E), BF16)
    row = pltpu.VMEM((1, E), I32)
    out, slip, state = pl.pallas_call(
        kernel,
        out_shape=(
            jax.ShapeDtypeStruct((Q, B, E), F32),
            jax.ShapeDtypeStruct((FB, E), F32),
            jax.ShapeDtypeStruct((FB, E), F32),
        ),
        in_specs=[hbm] * 14,
        out_specs=(vmem,) * 3,
        scratch_shapes=[
            pltpu.VMEM((3, B, B), F32),
            pltpu.VMEM((FB, NF, B), F32),
            pltpu.VMEM((FB, NF, B), F32),
            pltpu.VMEM((NF, E), I32),
            pltpu.VMEM((NF, E), I32),
            row, row, row, row,
            pltpu.VMEM((3, FB, E), F32),
            pltpu.VMEM((FB, E), F32),
            pltpu.VMEM((ORD, Q, B, E), F32),
            pltpu.VMEM((Q, Q, 3, E), F32),
            pltpu.VMEM((2, Q, Q, NF, E), F32),
            pltpu.VMEM((Q, 3 * B, E), F32),
            pltpu.VMEM((176, 128), F32),
            pltpu.VMEM((128, 128), F32),
            pltpu.VMEM((176, 256), BF16),
            pltpu.VMEM((176, 256), BF16),
            pltpu.VMEM((128, 256), BF16),
            pltpu.VMEM((96, 256), BF16),
            pltpu.VMEM((112, 256), BF16),
            square,
            square,
            pltpu.VMEM((NF * E, E), BF16),
            halo, halo, halo, halo,
            pltpu.VMEM((Q * 2 * B, NC * EXT), BF16),
            pltpu.VMEM((NF, NC * EXT, E), BF16),
            pltpu.VMEM((NF, Q * 2 * B, E), BF16),
            faces, faces, faces,
            pltpu.VMEM((128, E), F32),
            small, small, double, double, small, small,
            pltpu.SemaphoreType.DMA((14,)),
            pltpu.SemaphoreType.DMA((2, ORD)),
            pltpu.SemaphoreType.DMA((2, ORD)),
            pltpu.SemaphoreType.DMA((3,)),
            pltpu.SemaphoreType.DMA((3,)),
            pltpu.SemaphoreType.DMA((3,)),
        ],
        compiler_params=pltpu.CompilerParams(
            collective_id=0, has_side_effects=True, vmem_limit_bytes=48 * 1024 * 1024
        ),
    )(*[pltpu.with_memory_space_constraint(v, pltpu.HBM) for v in (
        jnp.transpose(elem_dofs, (1, 0, 2)),
        jnp.transpose(star_mats, (1, 2, 0, 3)),
        jnp.transpose(flux_solver, (0, 2, 3, 1, 4)),
        stiffness,
        jnp.transpose(face_proj, (1, 0, 2)),
        jnp.transpose(lift_mats, (2, 0, 1)),
        neighbours,
        neighbour_face,
        cluster.reshape(1, E),
        fault_elem.reshape(1, E),
        fault_face.reshape(1, E),
        fault_target.reshape(1, E),
        fault_params,
        fault_state,
    )])
    return jnp.transpose(out, (1, 0, 2)), slip, state


def solution(mesh):
    return jax.shard_map(
        local,
        mesh=mesh,
        in_specs=(
            P(None, None, "dom"),
            P(None, None, None, "dom"),
            P(None, None, None, None, "dom"),
            P(),
            P(),
            P(),
            P(None, "dom"),
            P(None, "dom"),
            P("dom"),
            P("dom"),
            P("dom"),
            P("dom"),
            P(None, None, "dom"),
            P(None, "dom"),
        ),
        out_specs=(P(None, None, "dom"), P(None, "dom"), P(None, "dom")),
        check_vma=False,
    )
```

```python
import functools

import jax
import jax.numpy as jnp
from jax import lax
from jax.experimental import pallas as pl
from jax.experimental.pallas import tpu as pltpu
from jax.sharding import PartitionSpec as P

F32, BF16, I32 = jnp.float32, jnp.bfloat16, jnp.int32
MESH = pl.DeviceIdType.MESH
B, Q, FB, ORD, NF, NC, NEWTON = 56, 9, 21, 6, 4, 4, 4
E, RIM = 256, 64
N = 128
ORDER = (0, 3, 7, 1, 2, 4, 5, 6, 8)
FIRST = 3 * 2 * B
GP = 32
EXT = 384
BASE_STEP, STEADY = 0.2, 0.8
TAUS = [BASE_STEP * 2.0**c for c in range(NC)]


def term_weights(tau):
    out, weight = [], 1.0
    for degree in range(ORD):
        weight = weight * tau / (degree + 1)
        out.append(weight)
    return out


WEIGHTS = [term_weights(tau) for tau in TAUS]


def iota(shape, dim):
    return lax.broadcasted_iota(I32, shape, dim)


def dot(a, b):
    return jnp.dot(a, b, preferred_element_type=F32)


def dot_nt(a, b):
    return lax.dot_general(a, b, (((1,), (1,)), ((), ())), preferred_element_type=F32)


def split2(x):
    high = x.astype(BF16).astype(F32)
    return high, x - high


def pieces(x):
    high = x.astype(BF16)
    return high, (x - high.astype(F32)).astype(BF16)


def stacked(x):
    high, low = split2(x)
    gap = jnp.zeros((8, x.shape[1]), F32)
    half = jnp.concatenate([high, gap, low, gap], axis=0).astype(BF16)
    return jnp.concatenate([half, half], axis=0)


def left_factor(w):
    both = w + pltpu.roll(w, 64, axis=1)
    high, low = split2(both)
    return jnp.concatenate([high.astype(BF16), low.astype(BF16)], axis=1)


def inverse_sinh(value):
    magnitude = jnp.abs(value)
    result = jnp.log(magnitude + jnp.sqrt(1.0 + magnitude * magnitude))
    return jnp.where(value < 0.0, -result, result)


def kernel(
    dofs_h, star_h, flux_h, *rest
):
    small_h, rest = rest[:11], rest[11:]
    (acc, slip_out, state_out), rest = rest[:3], rest[3:]
    small_v, rest = rest[:11], rest[11:]
    stiff, proj, lift, nbr, nbr_face, cluster, f_elem, f_face, f_target, params, state = small_v
    (x, star, flux, st, wide, pad_sq, s4, st4, f4, f4b, l2, mem, own_of, etab,
    hsl, hsr, hrl, hrr, amat, gmat, y, of, nb, fx, pp,
    bq, rq, bp, rp, bs, rs,
    in_sem, hs_sem, hr_sem, ex_s, ex_r, ex_o) = rest
    me = lax.axis_index("dom")
    n = N
    left, right = (me + n - 1) % n, (me + 1) % n

    in_copies = [
        pltpu.make_async_copy(dofs_h, x.at[0], in_sem.at[0]),
        pltpu.make_async_copy(star_h, star, in_sem.at[1]),
        pltpu.make_async_copy(flux_h, flux, in_sem.at[2]),
    ]
    small_copies = [
        pltpu.make_async_copy(source, place, in_sem.at[3 + i])
        for i, (source, place) in enumerate(zip(small_h, small_v))
    ]
    for copy in small_copies + in_copies:
        copy.start()

    barrier = pltpu.get_barrier_semaphore()

    def others(action):
        def one(t, _):
            action(t)
            return 0

        lax.fori_loop(me + 1, n, one, 0)
        lax.fori_loop(0, me, one, 0)

    others(lambda t: pl.semaphore_signal(barrier, inc=1, device_id=(t,), device_id_type=MESH))

    def row_copy(buf, dst, rows, which, t):
        return pltpu.make_async_remote_copy(
            src_ref=buf.at[pl.ds(t * rows, rows)],
            dst_ref=dst.at[pl.ds(me * rows, rows)],
            send_sem=ex_s.at[which], recv_sem=ex_r.at[which],
            device_id=(t,), device_id_type=MESH,
        )

    def send(buf, dst, rows, which):
        others(lambda t: row_copy(buf, dst, rows, which, t).start())
        pltpu.make_async_copy(buf.at[pl.ds(me * rows, rows)], dst.at[pl.ds(me * rows, rows)], ex_o.at[which]).start()

    def arrive(buf, dst, rows, which):
        pltpu.make_async_copy(buf.at[pl.ds(me * rows, rows)], dst.at[pl.ds(me * rows, rows)], ex_o.at[which]).wait()
        pltpu.make_async_copy(
            buf.at[pl.ds(0, (n - 1) * rows)], dst.at[pl.ds(0, (n - 1) * rows)], ex_r.at[which]
        ).wait()

    def sent(buf, dst, rows, which):
        pltpu.make_async_copy(
            buf.at[pl.ds(0, (n - 1) * rows)], dst.at[pl.ds(0, (n - 1) * rows)], ex_s.at[which]
        ).wait()

    def halo_copies(k):
        return (
            pltpu.make_async_remote_copy(
                src_ref=hsl.at[k], dst_ref=hrr.at[k], send_sem=hs_sem.at[0, k], recv_sem=hr_sem.at[0, k],
                device_id=(left,), device_id_type=MESH),
            pltpu.make_async_remote_copy(
                src_ref=hsr.at[k], dst_ref=hrl.at[k], send_sem=hs_sem.at[1, k], recv_sem=hr_sem.at[1, k],
                device_id=(right,), device_id_type=MESH),
        )

    for copy in small_copies:
        copy.wait()
    wide[...] = jnp.zeros_like(wide)
    for d in range(3):
        wide[d * B : (d + 1) * B, 0:B] = stiff[d]
    s4[...] = left_factor(wide[...])
    for d in range(3):
        pad_sq[...] = jnp.zeros_like(pad_sq)
        pad_sq[0:B, 0:B] = stiff[d]
        wide[d * B : (d + 1) * B, :] = jnp.transpose(pad_sq[...])[0:B]
    st4[...] = left_factor(wide[...])
    pad_sq[...] = jnp.zeros_like(pad_sq)
    for f in range(NF):
        pad_sq[f * GP : f * GP + FB, 0:B] = proj[:, f, :]
    f4[...] = left_factor(pad_sq[...])
    pad_sq[...] = jnp.zeros_like(pad_sq)
    for f in range(NF):
        pad_sq[f * 24 : f * 24 + FB, 0:B] = proj[:, f, :]
    high, low = [jnp.concatenate([v, jnp.zeros((96, 128), F32)], axis=1) for v in split2(pad_sq[0:96, :])]
    f4b[...] = (
        high + pltpu.roll(high, B, axis=1) + pltpu.roll(low, 2 * B, axis=1) + pltpu.roll(low, 3 * B, axis=1)
    ).astype(BF16)
    pad_sq[...] = jnp.zeros_like(pad_sq)
    for f in range(NF):
        pad_sq[f * GP : f * GP + FB, 0:B] = lift[:, f, :]
    lift_high, lift_low = split2(jnp.transpose(pad_sq[...])[0:B])
    lift_rows = jnp.concatenate([lift_high, lift_low], axis=0).astype(BF16)
    l2[...] = jnp.concatenate([lift_rows, lift_rows], axis=1)
    fx[...] = jnp.zeros_like(fx)
    pp[...] = jnp.zeros_like(pp)
    for j in range(3):
        pp[24 * j : 24 * j + FB, :] = params[j]
    pp[72 : 72 + FB, :] = state[...]

    target = f_target[...]
    live = target >= 0
    owner = jnp.where(live, lax.shift_right_logical(target, 8), -1)
    slot = jnp.bitwise_and(target, E - 1)
    member = jnp.where(iota((n, E), 0) == owner, 1.0, 0.0)
    earlier = jnp.where(iota((E, E), 0) < iota((E, E), 1), 1.0, 0.0).astype(BF16)
    before = dot(member.astype(BF16), earlier)
    rank = jnp.sum(member * before, axis=0, keepdims=True)
    place = owner.astype(F32) + n * rank
    place = jnp.where(live, place, -1.0)
    mem[...] = jnp.where(iota((E, E), 0).astype(F32) == place, 1.0, 0.0).astype(BF16)
    grid_place = jnp.where(live, f_face[...] * E + f_elem[...], -1)
    for f in range(NF):
        etab[f * E : (f + 1) * E, :] = jnp.where(iota((E, E), 0) + f * E == grid_place, 1.0, 0.0).astype(BF16)
    ids = jnp.where(iota((128, E), 0) < 2, (slot + 1).astype(F32), 0.0).astype(BF16)
    asked = dot_nt(mem[...], ids)
    lane2 = iota((n, 128), 1)
    bq[...] = jnp.where(lane2 == 0, asked[0:n], asked[n : 2 * n])

    lane = iota((32, 128), 1)
    low_half = lane < RIM

    def pack_halo(k, q, half, value):
        if half == 0:
            hsl[k, q] = jnp.where(low_half, value[0:32], pltpu.roll(value[24:56], RIM, axis=1))
        else:
            hsr[k, q] = jnp.where(low_half, pltpu.roll(value[0:32], RIM, axis=1), value[24:56])

    def send_halo(k):
        for copy in halo_copies(k):
            copy.start()

    def star_products(left_w, source):
        def one(q, _):
            st[q] = dot(left_w[...], stacked(source(q)))[0 : 3 * B]
            return 0

        lax.fori_loop(0, Q, one, 0, unroll=True)

    def star_sum(store):
        def one(g, _):
            for l in range(2):
                lanes = slice(l * 128, (l + 1) * 128)
                total = [jnp.zeros((B, 128), F32) for _ in range(3)]
                for q in range(Q):
                    for d in range(3):
                        value = st[q, d * B : (d + 1) * B, lanes]
                        for i in range(3):
                            total[i] = total[i] + star[g * 3 + i, q, d : d + 1, lanes] * value
                for i in range(3):
                    store(g * 3 + i, l, lanes, total[i])
            return 0

        lax.fori_loop(0, 3, one, 0)

    def taylor(k):
        star_products(s4, lambda q: x[k - 1, q])

        def store(p, l, lanes, value):
            x[k, p, :, lanes] = value
            pack_halo(k, p, l, value)

        star_sum(store)

    for copy in in_copies[:2]:
        copy.wait()
    for q in range(Q):
        for l in range(2):
            pack_halo(0, q, l, x[0, q, :, l * 128 : (l + 1) * 128])
    taylor(1)
    pl.semaphore_wait(barrier, n - 1)
    send_halo(0)
    send(bq, rq, 1, 0)
    send_halo(1)
    for k in range(2, ORD - 1):
        taylor(k)
        send_halo(k)

    taylor(ORD - 1)
    send_halo(ORD - 1)

    level = cluster[...]

    def by_level(values):
        out = jnp.full((1, E), values[0], F32)
        for c in range(1, NC):
            out = jnp.where(level == c, values[c], out)
        return out

    step = by_level(TAUS)
    own_w = [by_level([WEIGHTS[c][k] for c in range(NC)]) for k in range(ORD)]

    def own_term(q, _):
        total = own_w[0] * x[0, q]
        for k in range(1, ORD):
            total = total + own_w[k] * x[k, q]
        wrapped = stacked(total)
        st[q] = dot(st4[...], wrapped)[0 : 3 * B]
        of[q] = dot(f4[...], wrapped)
        return 0

    lax.fori_loop(0, Q, own_term, 0, unroll=3)

    arrive(bq, rq, 1, 0)
    wanted = (iota((n, E), 1) + 1).astype(F32)
    for r in range(2):
        own_of[r * n : (r + 1) * n, :] = jnp.where(rq[:, r : r + 1] == wanted, 1.0, 0.0).astype(BF16)
    answer = sum(dot_nt(own_of[...], piece) for piece in pieces(pp[...]))
    for r in range(2):
        bp[pl.ds(r, n, stride=2), :] = answer[r * n : (r + 1) * n]
    send(bp, rp, 2, 1)
    number = nbr[...] - me * E
    ext = jnp.where(number < RIM, number + E, jnp.where(number >= E + RIM, number, number - RIM))
    column = level * EXT + ext
    for f in range(NF):
        def build(c, _, f=f):
            rows = pl.ds(pl.multiple_of(c * E, E), E)
            hit = iota((E, E), 0) + c * E == column[f : f + 1]
            gmat[f, rows, :] = jnp.where(hit, 1.0, 0.0).astype(BF16)
            return 0

        lax.fori_loop(0, NC * EXT // E, build, 0)

    def cluster_sums(terms, row, l):
        for c in range(NC):
            total = WEIGHTS[c][0] * terms[0]
            for k in range(1, ORD):
                total = total + WEIGHTS[c][k] * terms[k]
            high, low = split2(total)
            rows = slice(row * 2 * B, (row + 1) * 2 * B)
            lanes = slice(c * EXT + l * 128, c * EXT + (l + 1) * 128)
            amat[rows, lanes] = jnp.concatenate([high, low], axis=0).astype(BF16)

    for q in range(Q):
        for l in range(2):
            cluster_sums([x[k, q, :, l * 128 : (l + 1) * 128] for k in range(ORD)], ORDER.index(q), l)

    keep_low = jnp.where(me > 0, 1, 0)
    keep_high = jnp.where(me < n - 1, 1, 0)
    keep = jnp.where(lane < RIM, keep_low, keep_high) > 0
    for k in range(ORD):
        for copy in halo_copies(k):
            copy.wait_recv()

    for q in range(Q):
        terms = []
        for k in range(ORD):
            a, b = hrl[k, q], hrr[k, q]
            top = jnp.where(keep, jnp.where(low_half, a, pltpu.roll(b, RIM, axis=1)), 0.0)
            bottom = jnp.where(keep, jnp.where(low_half, pltpu.roll(a, RIM, axis=1), b), 0.0)
            terms.append(jnp.concatenate([top, bottom[8:32]], axis=0))
        cluster_sums(terms, ORDER.index(q), 2)

    def gather(start, stop):
        def one(f, _):
            y[f, start:stop, :] = dot(amat[start:stop, :], gmat[f]).astype(BF16)
            return 0

        lax.fori_loop(0, NF, one, 0)

    def project(q):
        start = ORDER.index(q) * 2 * B
        for f in range(NF):
            side = nbr_face[f : f + 1, :]
            half = y[f, start : start + 2 * B, :]
            table = dot(f4b[...], jnp.concatenate([half, half, jnp.zeros((32, E), BF16)], axis=0))
            picked = table[0:24]
            for s in range(1, NF):
                picked = jnp.where(side == s, table[s * 24 : (s + 1) * 24], picked)
            nb[q, f * GP : f * GP + 24, :] = picked

    gather(0, FIRST)
    for q in ORDER[:3]:
        project(q)

    arrive(bp, rp, 2, 1)
    given = jnp.concatenate([rp[pl.ds(r, n, stride=2), :] for r in range(2)], axis=0)
    by_slot = sum(dot(piece, mem[...]) for piece in pieces(jnp.transpose(given)))
    by_slot = jnp.where(iota((128, E), 0) == 96, 1.0, by_slot)
    slot_state = by_slot[72:96]
    slot_pieces = pieces(by_slot)
    slips = []
    for f in range(NF):
        table = etab[f * E : (f + 1) * E, :]
        grid = sum(dot_nt(piece, table) for piece in slot_pieces)
        rate, stress, imp, var = grid[0:24], grid[24:48], grid[48:72], grid[72:96]
        here = grid[96:97] > 0.5
        imp = jnp.where(imp > 0.0, imp, 1.0)
        rows = slice(f * GP, f * GP + 24)
        inner = [of[p, rows, :] / step for p in (0, 3, 7)]
        outer = [nb[p, rows, :] / step for p in (0, 3, 7)]
        locked = 0.5 * (inner[1] + outer[1]) + imp * (outer[2] - inner[2])
        normal = jnp.maximum(stress - 0.5 * (inner[0] + outer[0]), 1.0)
        strength = normal * rate
        gain = 0.5 * jnp.exp(var)
        slip = jnp.zeros_like(locked)
        for _ in range(NEWTON):
            scaled = gain * slip
            mismatch = imp * slip + strength * inverse_sinh(scaled) - locked
            tangent = imp + strength * gain / jnp.sqrt(1.0 + scaled * scaled)
            slip = slip - mismatch / tangent
        traction = locked - imp * slip
        nb[3, rows, :] = jnp.where(here, step * traction, nb[3, rows, :])
        nb[7, rows, :] = jnp.where(here, step * (inner[2] + slip), nb[7, rows, :])
        slips.append(pieces(jnp.where(here, slip, 0.0)))
    slot_slip = jnp.zeros((24, E), F32)
    for f in range(NF):
        for piece in slips[f]:
            slot_slip = slot_slip + dot(piece, etab[f * E : (f + 1) * E, :])
    slip_out[...] = slot_slip[0:FB]
    next_state = STEADY + (slot_state - STEADY) * jnp.exp(-jnp.abs(slot_slip))
    gap8, gap72 = jnp.zeros((8, E), F32), jnp.zeros((72, E), F32)
    wrapped = jnp.concatenate([next_state, gap8, next_state, gap72], axis=0)
    told = sum(dot_nt(mem[...], piece) for piece in pieces(wrapped))
    bs[...] = jnp.where(lane2 < 32, told[0:n], told[n : 2 * n])
    send(bs, rs, 1, 2)

    gather(FIRST, Q * 2 * B)
    for q in ORDER[3:]:
        project(q)

    def store_volume(p, _, lanes, value):
        acc[p, :, lanes] = x[0, p, :, lanes] + value

    star_sum(store_volume)

    in_copies[2].wait()

    def fluxes(g, _):
        for l in range(2):
            lanes = slice(l * 128, (l + 1) * 128)
            for f in range(NF):
                rows = slice(f * GP, f * GP + 24)
                total = [jnp.zeros((24, 128), F32) for _ in range(3)]
                for q in range(Q):
                    mine, other = of[q, rows, lanes], nb[q, rows, lanes]
                    for i in range(3):
                        total[i] = total[i] + flux[0, g * 3 + i, q, f : f + 1, lanes] * mine
                        total[i] = total[i] + flux[1, g * 3 + i, q, f : f + 1, lanes] * other
                for i in range(3):
                    fx[g * 3 + i, rows, lanes] = total[i]
        return 0

    lax.fori_loop(0, 3, fluxes, 0)

    def lifted(p, _):
        high, low = split2(fx[p])
        both = jnp.concatenate([high, low], axis=0).astype(BF16)
        surface = dot(l2[...], both)
        acc[p] = acc[p] - (surface[0:B] + surface[B : 2 * B])
        return 0

    lax.fori_loop(0, Q, lifted, 0, unroll=True)
    arrive(bs, rs, 1, 2)
    turned = jnp.transpose(rs[...])
    news = jnp.concatenate([turned[0:24], turned[32:56]], axis=1)
    update = sum(dot(piece, own_of[...]) for piece in pieces(news))
    hit = dot(jnp.ones((16, E), BF16), own_of[...])[0:1] > 0.5
    state_out[...] = jnp.where(hit, update[0:FB], state[...])

    sent(bq, rq, 1, 0)
    sent(bp, rp, 2, 1)
    sent(bs, rs, 1, 2)
    for k in range(ORD):
        for copy in halo_copies(k):
            copy.wait_send()


def local(*args):
    (elem_dofs, star_mats, flux_solver, stiffness, face_proj, lift_mats, neighbours, neighbour_face,
     cluster, fault_elem, fault_face, fault_target, fault_params, fault_state) = args
    vmem, hbm = pl.BlockSpec(memory_space=pltpu.VMEM), pl.BlockSpec(memory_space=pltpu.HBM)
    halo = pltpu.VMEM((ORD, Q, 32, 128), F32)
    small = pltpu.VMEM((N, 128), F32)
    double = pltpu.VMEM((2 * N, 128), F32)
    faces = pltpu.VMEM((Q, NF * GP, E), F32)
    square = pltpu.VMEM((E, E), BF16)
    row = pltpu.VMEM((1, E), I32)
    out, slip, state = pl.pallas_call(
        kernel,
        out_shape=(
            jax.ShapeDtypeStruct((Q, B, E), F32),
            jax.ShapeDtypeStruct((FB, E), F32),
            jax.ShapeDtypeStruct((FB, E), F32),
        ),
        in_specs=[hbm] * 14,
        out_specs=(vmem,) * 3,
        scratch_shapes=[
            pltpu.VMEM((3, B, B), F32),
            pltpu.VMEM((FB, NF, B), F32),
            pltpu.VMEM((FB, NF, B), F32),
            pltpu.VMEM((NF, E), I32),
            pltpu.VMEM((NF, E), I32),
            row, row, row, row,
            pltpu.VMEM((3, FB, E), F32),
            pltpu.VMEM((FB, E), F32),
            pltpu.VMEM((ORD, Q, B, E), F32),
            pltpu.VMEM((Q, Q, 3, E), F32),
            pltpu.VMEM((2, Q, Q, NF, E), F32),
            pltpu.VMEM((Q, 3 * B, E), F32),
            pltpu.VMEM((176, 128), F32),
            pltpu.VMEM((128, 128), F32),
            pltpu.VMEM((176, 256), BF16),
            pltpu.VMEM((176, 256), BF16),
            pltpu.VMEM((128, 256), BF16),
            pltpu.VMEM((96, 256), BF16),
            pltpu.VMEM((112, 256), BF16),
            square,
            square,
            pltpu.VMEM((NF * E, E), BF16),
            halo, halo, halo, halo,
            pltpu.VMEM((Q * 2 * B, NC * EXT), BF16),
            pltpu.VMEM((NF, NC * EXT, E), BF16),
            pltpu.VMEM((NF, Q * 2 * B, E), BF16),
            faces, faces, faces,
            pltpu.VMEM((128, E), F32),
            small, small, double, double, small, small,
            pltpu.SemaphoreType.DMA((14,)),
            pltpu.SemaphoreType.DMA((2, ORD)),
            pltpu.SemaphoreType.DMA((2, ORD)),
            pltpu.SemaphoreType.DMA((3,)),
            pltpu.SemaphoreType.DMA((3,)),
            pltpu.SemaphoreType.DMA((3,)),
        ],
        compiler_params=pltpu.CompilerParams(
            collective_id=0, has_side_effects=True, vmem_limit_bytes=48 * 1024 * 1024
        ),
    )(*[pltpu.with_memory_space_constraint(v, pltpu.HBM) for v in (
        jnp.transpose(elem_dofs, (1, 0, 2)),
        jnp.transpose(star_mats, (1, 2, 0, 3)),
        jnp.transpose(flux_solver, (0, 2, 3, 1, 4)),
        stiffness,
        jnp.transpose(face_proj, (1, 0, 2)),
        jnp.transpose(lift_mats, (2, 0, 1)),
        neighbours,
        neighbour_face,
        cluster.reshape(1, E),
        fault_elem.reshape(1, E),
        fault_face.reshape(1, E),
        fault_target.reshape(1, E),
        fault_params,
        fault_state,
    )])
    return jnp.transpose(out, (1, 0, 2)), slip, state


def solution(mesh):
    return jax.shard_map(
        local,
        mesh=mesh,
        in_specs=(
            P(None, None, "dom"),
            P(None, None, None, "dom"),
            P(None, None, None, None, "dom"),
            P(),
            P(),
            P(),
            P(None, "dom"),
            P(None, "dom"),
            P("dom"),
            P("dom"),
            P("dom"),
            P("dom"),
            P(None, None, "dom"),
            P(None, "dom"),
        ),
        out_specs=(P(None, None, "dom"), P(None, "dom"), P(None, "dom")),
        check_vma=False,
    )
```
